32 devices in a mesh: ctx: 8 (over z, y), head: 4 (over x, core).
Axes of the slice: x: 2, y: 2, z: 4, core: 2. Of those that a mesh axis runs over, the one named last changes fastest.
Arguments:
- lin_query: bfloat16 [1024, 6144], P('ctx', 'head'), may hold values from -6 to 6
- lin_key: bfloat16 [1024, 6144], P('ctx', 'head'), may hold values from -6 to 6
- lin_value: bfloat16 [1024, 6144], P('ctx', 'head'), may hold values from -6 to 6
- soft_query: bfloat16 [1024, 6144], P('ctx', 'head'), may hold values from -6 to 6
- soft_key: bfloat16 [1024, 6144], P('ctx', 'head'), may hold values from -6 to 6
- soft_value: bfloat16 [1024, 6144], P('ctx', 'head'), may hold values from -6 to 6
- upstream: bfloat16 [1024, 6144], P('ctx', 'head'), may hold values from -6 to 6
- doc_lengths: int32 [5], replicated, may hold values from 1 to 384, 1024 in all
- doc_domain: int32 [5], replicated, may hold values from 0 to 7
- domain_weight: float32 [8], replicated, may hold values from 0.25 to 4
Outputs:
- lin_dq: bfloat16 [1024, 6144], P('ctx', 'head')
- lin_dk: bfloat16 [1024, 6144], P('ctx', 'head')
- lin_dv: bfloat16 [1024, 6144], P('ctx', 'head')
- soft_dq: bfloat16 [1024, 6144], P('ctx', 'head')
- soft_dk: bfloat16 [1024, 6144], P('ctx', 'head')
- soft_dv: bfloat16 [1024, 6144], P('ctx', 'head')
- domain_loss: float32 [8], replicated
The draws below stay inside these ranges and needn't reach their ends.
Inputs may be any that keep to these rules, and one draw needn't show every extreme that they name: `doc_lengths`: whole documents fill the sequence in order; the longest has exactly 384 tokens.
All inputs are finite; a program needn't handle non-finite values.
Results may differ from the reference program's by a relative error of at most 0.029.
Values may be sent and summed in bfloat16 or wider, within the bound.
A program may use at most 192 MiB of HBM per device.

```python
import math
import jax
import jax.numpy as jnp
import numpy as np
from jax import lax

HEADS = 48
HD = 128
TOK_DEV = 128
REACH = 3
NDOM = 8
SEQ = 1024
DOC_MOST = 384
NDOCS = 5
N_CTX = 8


def soft_pair(key):
    base = jax.random.fold_in(key, 11)
    first_key, second_key = jax.random.split(base, 2)
    shape = (SEQ, HEADS * HD)
    queries = jnp.clip(jax.random.normal(first_key, shape, jnp.float32), -6.0, 6.0)
    keyset = jnp.clip(jax.random.normal(second_key, shape, jnp.float32), -6.0, 6.0)
    return (queries, keyset)


def draw_soft_query(key, part):
    queries, keyset = soft_pair(key)
    return queries.astype(jnp.bfloat16)


def draw_soft_key(key, part):
    queries, keyset = soft_pair(key)
    return keyset.astype(jnp.bfloat16)


def place_ends(entries, rng, least, largest):
    dims = entries.shape
    index_at = [jax.random.randint(jax.random.fold_in(rng, axis), (), 0, dims[axis]) for axis in range(len(dims))]
    entries = entries.at[tuple(index_at)].set(least)
    longest = dims.index(max(dims))
    index_at[longest] = (index_at[longest] + 1) % dims[longest]
    return entries.at[tuple(index_at)].set(largest)


def steps_of(own_key, dims, cuts, smallest, largest):
    def one(position, parts):
        draws = jax.random.uniform(jax.random.fold_in(jax.random.fold_in(own_key, 6), position), (parts,), jnp.float32, smallest / len(cuts), largest / len(cuts))
        return jnp.repeat(jnp.exp(draws), dims[position] // parts).reshape((-1,) + (1,) * (len(dims) - position - 1))

    level = one(*cuts[0])
    for cut in cuts[1:]:
        level = level * one(*cut)
    return level


def split_up(amount, total, limit, slope):
    weights = [(1 << 20) // math.isqrt(rank ** slope) + 1 for rank in range(2, amount + 1)]
    rest, given = total - limit - (amount - 1), [1] * (amount - 1)
    while rest > 0:
        movable = [i for i in range(amount - 1) if given[i] < limit]
        pool, left = sum([weights[i] for i in movable]), rest
        for i in movable:
            more = min(limit - given[i], max(1, left * weights[i] // pool), rest)
            given[i] = given[i] + more
            rest = rest - more
    return np.array([limit] + given)


def ragged_sizes(own_key, amount, total, limit, slope):
    if amount == 2:
        one = jax.random.randint(own_key, (), max(1, total - limit), min(limit, total - 1) + 1)
        return jnp.stack([one, total - one])
    sizes = jnp.asarray(split_up(amount, total, limit, slope), jnp.int32)
    twos = (amount - 1) // 2
    source_of, taker = sizes[1:1 + 2 * twos:2], sizes[2:2 + 2 * twos:2]
    margin = jnp.minimum(source_of - 1, limit - taker)
    passed = jax.random.randint(jax.random.fold_in(own_key, 1), (twos,), 0, 1 << 20) % (margin + 1)
    sizes = sizes.at[1:1 + 2 * twos:2].set(source_of - passed).at[2:2 + 2 * twos:2].set(taker + passed)
    return sizes[jax.random.permutation(jax.random.fold_in(own_key, 2), amount)]


def gaussian(key, dims, spread, limit, cuts=(), held_as=jnp.bfloat16):
    entries = jax.random.normal(key, dims, jnp.float32) * spread
    if len(cuts) > 0:
        entries = steps_of(key, dims, cuts, -0.22, 0.18) * entries
    return jnp.clip(entries, min=-limit, max=limit).astype(held_as)


def setup_inputs(seed: int = 0) -> dict:
    streams_of = jax.random.split(jax.random.key(seed), 11)
    lin_query = gaussian(streams_of[0], (SEQ, HEADS * HD), 1.0, 6.0, ((0, 8), (1, 4)))
    lin_key = gaussian(streams_of[1], (SEQ, HEADS * HD), 1.0, 6.0, ((0, 8), (1, 4)))
    lin_value = gaussian(streams_of[2], (SEQ, HEADS * HD), 1.0, 6.0, ((0, 8), (1, 4)))
    soft_query = draw_soft_query(jax.random.fold_in(streams_of[10], 71), 0)
    soft_key = draw_soft_key(jax.random.fold_in(streams_of[10], 71), 0)
    soft_value = gaussian(streams_of[5], (SEQ, HEADS * HD), 1.0, 6.0, ((0, 8), (1, 4)))
    upstream = gaussian(streams_of[6], (SEQ, HEADS * HD), 1.0, 6.0, ((0, 8), (1, 4)))
    doc_lengths = ragged_sizes(streams_of[7], NDOCS, SEQ, DOC_MOST, 2).astype(jnp.int32)
    doc_domain = place_ends(jax.random.randint(streams_of[8], (NDOCS,), 0, NDOM), jax.random.fold_in(streams_of[8], 1), 0, NDOM - 1).astype(jnp.int32)
    domain_weight = jnp.clip(jnp.exp(jax.random.uniform(streams_of[9], (NDOM,), jnp.float32, math.log(0.25), math.log(4.0))), 0.25, 4.0)
    return {"lin_query": lin_query, "lin_key": lin_key, "lin_value": lin_value, "soft_query": soft_query, "soft_key": soft_key, "soft_value": soft_value, "upstream": upstream, "doc_lengths": doc_lengths, "doc_domain": doc_domain, "domain_weight": domain_weight}


def token_docs(doc_lengths, positions):
    doc_ends = jnp.cumsum(doc_lengths).astype(jnp.int32)
    doc_starts = (doc_ends - doc_lengths).astype(jnp.int32)
    inside = (doc_starts[None, :] <= positions[:, None]) & (positions[:, None] < doc_ends[None, :])
    numbers = jnp.arange(1, doc_lengths.shape[0] + 1, dtype=jnp.int32)
    doc_index = (jnp.sum(jnp.where(inside, numbers[None, :], 0), axis=1) - 1).astype(jnp.int32)
    doc_begin = jnp.sum(jnp.where(inside, doc_starts[None, :], 0), axis=1).astype(jnp.int32)
    doc_finish = jnp.sum(jnp.where(inside, doc_ends[None, :], 0), axis=1).astype(jnp.int32)
    return inside, doc_index, doc_begin, doc_finish


def token_weights(inside, doc_domain, domain_weight):
    domain_of = jnp.sum(jnp.where(inside, doc_domain[None, :], 0), axis=1).astype(jnp.int32)
    domain_ids = jnp.arange(domain_weight.shape[0], dtype=jnp.int32)
    domain_hot = (domain_of[:, None] == domain_ids[None, :]).astype(jnp.float32)
    return jnp.sum(domain_hot * domain_weight[None, :], axis=1), domain_hot


def reference(lin_query, lin_key, lin_value, soft_query, soft_key, soft_value, upstream, doc_lengths, doc_domain, domain_weight):
    feat_cols = HEADS * HD
    linear_scale = (HD * DOC_MOST) ** -0.5
    soft_scale = HD ** -0.5
    highest_index = lax.Precision.HIGHEST
    positions = jnp.arange(SEQ, dtype=jnp.int32)
    inside, doc_index, doc_begin, doc_finish = token_docs(doc_lengths, positions)
    weights, domain_hot = token_weights(inside, doc_domain, domain_weight)
    grad_out = (weights[:, None] * upstream.astype(jnp.float32)).astype(jnp.bfloat16)

    def blocked(array):
        return array.reshape(N_CTX, TOK_DEV, HEADS, HD)

    query_b, key_b, value_b, grad_b = blocked(lin_query), blocked(lin_key), blocked(lin_value), blocked(grad_out)
    index_b = doc_index.reshape(N_CTX, TOK_DEV)
    begin_b = doc_begin.reshape(N_CTX, TOK_DEV)
    finish_b = doc_finish.reshape(N_CTX, TOK_DEV)
    block_ids = jnp.arange(N_CTX, dtype=jnp.int32)
    order = jnp.arange(TOK_DEV, dtype=jnp.int32)

    def local_scores(query_rows, key_rows, value_rows, gradient_heads, ids):
        allowed = (ids[:, None] == ids[None, :]) & (order[None, :] <= order[:, None])
        lin_scores = jnp.where(allowed[None], linear_scale * jnp.einsum('thd,shd->hts', query_rows.astype(jnp.float32), key_rows.astype(jnp.float32)), 0.0).astype(jnp.bfloat16)
        lin_back = jnp.where(allowed[None], linear_scale * jnp.einsum('thd,shd->hts', gradient_heads.astype(jnp.float32), value_rows.astype(jnp.float32)), 0.0).astype(jnp.bfloat16)
        return lin_scores, lin_back

    def forward_step(summed_state, inputs):
        query_rows, key_rows, value_rows, gradient_heads, ids, begins, block = inputs
        row_start = block * TOK_DEV
        lin_scores, lin_back = local_scores(query_rows, key_rows, value_rows, gradient_heads, ids)
        carried_along = (begins < row_start).astype(jnp.float32)[:, None, None]
        inner = jnp.einsum('hts,shd->thd', lin_scores.astype(jnp.float32), value_rows.astype(jnp.float32))
        outer_product = linear_scale * carried_along * jnp.einsum('jlb,lbw->jlw', query_rows.astype(jnp.float32), summed_state, precision=highest_index)
        lin_out = (inner + outer_product).astype(jnp.bfloat16)
        dq_inner = jnp.einsum('hts,shd->thd', lin_back.astype(jnp.float32), key_rows.astype(jnp.float32))
        outer_query_gradient = linear_scale * carried_along * jnp.einsum('nmu,meu->nme', gradient_heads.astype(jnp.float32), summed_state, precision=highest_index)
        lin_dq = (dq_inner + outer_query_gradient).astype(jnp.bfloat16)
        last_onehot = (ids == ids[TOK_DEV - 1]).astype(jnp.float32)[:, None, None]
        local_state = jnp.einsum('lzd,lzj->zdj', key_rows.astype(jnp.float32) * last_onehot, value_rows.astype(jnp.float32))
        flag = (begins[TOK_DEV - 1] >= row_start).astype(jnp.float32)
        return local_state + (1.0 - flag) * summed_state, (lin_out, lin_dq)

    zero_state = jnp.zeros((HEADS, HD, HD), jnp.float32)
    _, (lin_out_b, lin_dq_b) = lax.scan(forward_step, zero_state, (query_b, key_b, value_b, grad_b, index_b, begin_b, block_ids))

    def backward_step(summed_state, inputs):
        query_rows, key_rows, value_rows, gradient_heads, ids, finishes, block = inputs
        row_end = (block + 1) * TOK_DEV
        lin_scores, lin_back = local_scores(query_rows, key_rows, value_rows, gradient_heads, ids)
        extended_rows = (finishes > row_end).astype(jnp.float32)[:, None, None]
        dk_inner = jnp.einsum('hts,thd->shd', lin_back.astype(jnp.float32), query_rows.astype(jnp.float32))
        outer_key_gradient = linear_scale * extended_rows * jnp.einsum('mdx,dwx->mdw', value_rows.astype(jnp.float32), summed_state, precision=highest_index)
        dv_inner = jnp.einsum('hts,thd->shd', lin_scores.astype(jnp.float32), gradient_heads.astype(jnp.float32))
        outer_value_gradient = linear_scale * extended_rows * jnp.einsum('nzt,zti->nzi', key_rows.astype(jnp.float32), summed_state, precision=highest_index)
        first_onehot = (ids == ids[0]).astype(jnp.float32)[:, None, None]
        local_state = jnp.einsum('cis,ciy->isy', query_rows.astype(jnp.float32) * first_onehot, gradient_heads.astype(jnp.float32))
        flag = (finishes[0] <= row_end).astype(jnp.float32)
        return local_state + (1.0 - flag) * summed_state, ((dk_inner + outer_key_gradient).astype(jnp.bfloat16), (dv_inner + outer_value_gradient).astype(jnp.bfloat16))

    _, (lin_dk_b, lin_dv_b) = lax.scan(backward_step, zero_state, (query_b, key_b, value_b, grad_b, index_b, finish_b, block_ids), reverse=True)

    pad_rows = REACH * TOK_DEV
    window_rows = (REACH + 1) * TOK_DEV
    key_pad = jnp.concatenate([jnp.zeros((pad_rows, feat_cols), jnp.bfloat16), soft_key], axis=0)
    value_pad = jnp.concatenate([jnp.zeros((pad_rows, feat_cols), jnp.bfloat16), soft_value], axis=0)
    soft_query_b = blocked(soft_query)

    def soft_step(grads_pad, inputs):
        query_rows, gradient_heads, ids, block = inputs
        row_start = (block * TOK_DEV).astype(jnp.int32)
        positions_q = row_start + order
        key_heads = lax.dynamic_slice_in_dim(key_pad, row_start, window_rows, 0).reshape(window_rows, HEADS, HD)
        value_heads = lax.dynamic_slice_in_dim(value_pad, row_start, window_rows, 0).reshape(window_rows, HEADS, HD)
        positions_k = (row_start - pad_rows + jnp.arange(window_rows, dtype=jnp.int32)).astype(jnp.int32)
        _, key_docs, _, _ = token_docs(doc_lengths, positions_k)
        allowed = (key_docs[None, :] == ids[:, None]) & (positions_k[None, :] <= positions_q[:, None]) & (positions_k[None, :] >= 0)
        scores = soft_scale * jnp.einsum('thd,shd->hts', query_rows.astype(jnp.float32), key_heads.astype(jnp.float32))
        scores = jnp.where(allowed[None], scores, -jnp.inf)
        row_max = jnp.max(scores, axis=2, keepdims=True)
        log_total = row_max + jnp.log(jnp.sum(jnp.exp(scores - row_max), axis=2, keepdims=True))
        soft_prob = jnp.exp(scores - log_total)
        soft_weights = soft_prob.astype(jnp.bfloat16)
        soft_out = jnp.einsum('hts,shd->thd', soft_weights.astype(jnp.float32), value_heads.astype(jnp.float32)).astype(jnp.bfloat16)
        delta = jnp.sum(gradient_heads.astype(jnp.float32) * soft_out.astype(jnp.float32), axis=2)
        grad_prob = jnp.einsum('thd,shd->hts', gradient_heads.astype(jnp.float32), value_heads.astype(jnp.float32))
        soft_ds = (soft_prob * (grad_prob - delta.T[:, :, None]) * soft_scale).astype(jnp.bfloat16)
        soft_dq = jnp.einsum('hts,shd->thd', soft_ds.astype(jnp.float32), key_heads.astype(jnp.float32)).astype(jnp.bfloat16)
        key_grad = jnp.einsum('hts,thd->shd', soft_ds.astype(jnp.float32), query_rows.astype(jnp.float32)).reshape(window_rows, feat_cols)
        value_grad = jnp.einsum('hts,thd->shd', soft_weights.astype(jnp.float32), gradient_heads.astype(jnp.float32)).reshape(window_rows, feat_cols)
        key_acc, value_acc = grads_pad
        key_acc = lax.dynamic_update_slice_in_dim(key_acc, lax.dynamic_slice_in_dim(key_acc, row_start, window_rows, 0) + key_grad, row_start, 0)
        value_acc = lax.dynamic_update_slice_in_dim(value_acc, lax.dynamic_slice_in_dim(value_acc, row_start, window_rows, 0) + value_grad, row_start, 0)
        return (key_acc, value_acc), (soft_out, soft_dq)

    zero_pad = jnp.zeros((SEQ + pad_rows, feat_cols), jnp.float32)
    (key_total, value_total), (soft_out_b, soft_dq_b) = lax.scan(soft_step, (zero_pad, zero_pad), (soft_query_b, grad_b, index_b, block_ids))

    lin_out = lin_out_b.reshape(SEQ, feat_cols)
    soft_out = soft_out_b.reshape(SEQ, feat_cols)
    contrib = weights * jnp.sum(upstream.astype(jnp.float32) * (lin_out.astype(jnp.float32) + soft_out.astype(jnp.float32)), axis=1)
    domain_loss = jnp.sum(contrib[:, None] * domain_hot, axis=0)
    return (lin_dq_b.reshape(SEQ, feat_cols), lin_dk_b.reshape(SEQ, feat_cols), lin_dv_b.reshape(SEQ, feat_cols),
            soft_dq_b.reshape(SEQ, feat_cols), key_total[pad_rows:].astype(jnp.bfloat16), value_total[pad_rows:].astype(jnp.bfloat16),
            domain_loss)
```

```python
import functools

import jax
import jax.numpy as jnp
from jax import lax
from jax.experimental import pallas as pl
from jax.experimental.pallas import tpu as pltpu
from jax.sharding import PartitionSpec as P

HD = 128
DOC_MOST = 384
REACH = 3
HEADS_CHUNK = 2
NEG = -1e30
F32 = jnp.float32
BF16 = jnp.bfloat16
MESH = pl.DeviceIdType.MESH


def mm(a, b, ca, cb):
    return lax.dot_general(a, b, (((ca,), (cb,)), ((), ())), preferred_element_type=F32)


def kernel(
    n_ctx, n_head,
    lq_ref, lk_ref, lv_ref, sq_ref, sk_ref, sv_ref, up_ref, len_ref, dom_ref, dw_ref,
    ldq_ref, ldk_ref, ldv_ref, sdq_ref, sdk_ref, sdv_ref, loss_ref,
    fwd, bwd, stat, bias, bias_later, begin_s, dom_s, w_s, carried_s, extended_s,
    dk_acc, dv_acc, loss_row, loss_lane, loss_ctx, loss_head,
    send_f, recv_f, send_b, recv_b, send_s, recv_s, send_c, recv_c, send_h, recv_h,
):
    rows, cols = lq_ref.shape
    chunks = fwd.shape[1]
    wide = fwd.shape[4]
    per = wide // HD
    n_docs = len_ref.shape[0]
    n_dom = dw_ref.shape[0]
    lin_scale = (HD * DOC_MOST) ** (-0.5)
    soft_scale = HD ** (-0.5)
    b = lax.axis_index("ctx")
    hd = lax.axis_index("head")
    side = lax.rem(b, 2)
    partner = b + 1 - 2 * side

    barrier = pltpu.get_barrier_semaphore()
    for k in range(1, n_ctx):
        pl.semaphore_signal(
            barrier, inc=1, device_id={"ctx": lax.rem(b + k, n_ctx)}, device_id_type=MESH
        )
    for k in range(1, n_head):
        pl.semaphore_signal(
            barrier, inc=1, device_id={"head": lax.rem(hd + k, n_head)}, device_id_type=MESH
        )

    pos0 = b * rows
    pos_row = pos0 + lax.broadcasted_iota(jnp.int32, (8, rows), 1)
    pos_col = pos0 + lax.broadcasted_iota(jnp.int32, (rows, HD), 0)
    last = pos0 + rows - 1
    zero = jnp.int32(0)
    begin_row, dom_row = jnp.zeros_like(pos_row), jnp.zeros_like(pos_row)
    begin_col, end_col = jnp.zeros_like(pos_col), jnp.zeros_like(pos_col)
    w_col = jnp.zeros(pos_col.shape, F32)
    begin_first, end_first, begin_last, end_last = zero, zero, zero, zero
    start = zero
    for d in range(n_docs):
        end = start + len_ref[d]
        domain = dom_ref[d]
        weight = dw_ref[domain]
        in_row = (pos_row >= start) & (pos_row < end)
        in_col = (pos_col >= start) & (pos_col < end)
        begin_row = jnp.where(in_row, start, begin_row)
        dom_row = jnp.where(in_row, domain, dom_row)
        begin_col = jnp.where(in_col, start, begin_col)
        end_col = jnp.where(in_col, end, end_col)
        w_col = jnp.where(in_col, weight, w_col)
        has_first = (start <= pos0) & (pos0 < end)
        has_last = (start <= last) & (last < end)
        begin_first = jnp.where(has_first, start, begin_first)
        end_first = jnp.where(has_first, end, end_first)
        begin_last = jnp.where(has_last, start, begin_last)
        end_last = jnp.where(has_last, end, end_last)
        start = end
    dom_s[...] = dom_row
    w_s[...] = w_col
    carried_s[...] = jnp.where(begin_col < pos0, lin_scale, 0.0).astype(F32)
    extended_s[...] = jnp.where(end_col > pos0 + rows, lin_scale, 0.0).astype(F32)
    last_doc = jnp.where(pos_col >= begin_last, 1.0, 0.0).astype(BF16)
    first_doc = jnp.where(pos_col < end_first, 1.0, 0.0).astype(BF16)
    key_pos = pos0 - REACH * rows + lax.broadcasted_iota(jnp.int32, ((REACH + 1) * rows, rows), 0)
    allowed = (key_pos >= begin_row[0:1, :]) & (key_pos <= pos_row[0:1, :])
    bias[...] = jnp.where(allowed, 0.0, NEG).astype(F32)
    for j in range(1, REACH + 1):
        query_pos = pos0 + j * rows + lax.broadcasted_iota(jnp.int32, (rows, rows), 1)
        bias_later[:, (j - 1) * rows:j * rows] = jnp.where(
            query_pos < end_col, 0.0, NEG
        ).astype(F32)
    loss_row[...] = jnp.zeros_like(loss_row)
    loss_lane[...] = jnp.zeros_like(loss_lane)

    for j in range(1, REACH + 1):
        @pl.when(b - j < 0)
        def _():
            fwd[j] = jnp.zeros(fwd.shape[1:], BF16)

        @pl.when(b + j >= n_ctx)
        def _():
            bwd[j] = jnp.zeros(bwd.shape[1:], BF16)
            stat[j] = jnp.zeros(stat.shape[1:], F32)

    def move(buf, send, recv, msg, c, source, target, device):
        return pltpu.make_async_remote_copy(
            src_ref=buf.at[source, c],
            dst_ref=buf.at[target, c],
            send_sem=send.at[msg, c],
            recv_sem=recv.at[target, c],
            device_id={"ctx": device},
            device_id_type=MESH,
        )

    up2, down2 = b + 2, b - 2
    has_up, has_down = b + 2 < n_ctx, b - 2 >= 0

    def f_move(msg, c, source, target, device):
        return move(fwd, send_f, recv_f, msg, c, source, target, device)

    def b_move(msg, c, source, target, device):
        return move(bwd, send_b, recv_b, msg, c, source, target, device)

    def stat_move(j, c, device):
        return pltpu.make_async_remote_copy(
            src_ref=stat.at[0, c],
            dst_ref=stat.at[j, c],
            send_sem=send_s.at[j, c],
            recv_sem=recv_s.at[j, c],
            device_id={"ctx": device},
            device_id_type=MESH,
        )

    def stage_own(c):
        for h in range(per):
            sl = slice(h * HD, (h + 1) * HD)
            at = pl.ds(pl.multiple_of(c * wide + h * HD, HD), HD)
            g = (w_s[...] * up_ref[:, at].astype(F32)).astype(BF16)
            fwd[0, c, 0, :, sl] = sk_ref[:, at]
            fwd[0, c, 1, :, sl] = sv_ref[:, at]
            fwd[0, c, 2, :, sl] = mm(lk_ref[:, at] * last_doc, lv_ref[:, at], 0, 0).astype(BF16)
            bwd[0, c, 0, :, sl] = sq_ref[:, at]
            bwd[0, c, 1, :, sl] = g
            bwd[0, c, 2, :, sl] = mm(lq_ref[:, at] * first_doc, g, 0, 0).astype(BF16)

    def send_own(c):
        @pl.when(has_up)
        def _():
            f_move(0, c, 0, 2, up2).start()

        @pl.when(has_down)
        def _():
            b_move(0, c, 0, 2, down2).start()

        @pl.when(side == 0)
        def _():
            f_move(1, c, 0, 1, partner).start()

        @pl.when(side == 1)
        def _():
            b_move(1, c, 0, 1, partner).start()

    def pass_across(c):
        @pl.when(has_down)
        def _():
            f_move(0, c, 0, 2, partner).wait_recv()

            @pl.when(side == 1)
            def _():
                f_move(1, c, 2, 1, partner).start()

        @pl.when(has_up)
        def _():
            b_move(0, c, 0, 2, partner).wait_recv()

            @pl.when(side == 0)
            def _():
                b_move(1, c, 2, 1, partner).start()

    def pass_on(c):
        @pl.when(b >= 1)
        def _():
            f_move(1, c, 0, 1, partner).wait_recv()

            @pl.when(has_up)
            def _():
                f_move(2, c, 1, 3, up2).start()

        @pl.when(b + 1 < n_ctx)
        def _():
            b_move(1, c, 0, 1, partner).wait_recv()

            @pl.when(has_down)
            def _():
                b_move(2, c, 1, 3, down2).start()

    def forward(c):
        @pl.when(b >= 3)
        def _():
            f_move(2, c, 1, 3, partner).wait_recv()

        @pl.when(b + 3 < n_ctx)
        def _():
            b_move(2, c, 1, 3, partner).wait_recv()

        lse_rows, delta_rows = [], []
        for h in range(per):
            sl = slice(h * HD, (h + 1) * HD)
            at = pl.ds(pl.multiple_of(c * wide + h * HD, HD), HD)
            keys = jnp.concatenate([fwd[j, c, 0, :, sl] for j in (3, 2, 1, 0)], axis=0)
            values = jnp.concatenate([fwd[j, c, 1, :, sl] for j in (3, 2, 1, 0)], axis=0)
            q = bwd[0, c, 0, :, sl]
            g = bwd[0, c, 1, :, sl]
            scores = mm(keys, q, 1, 1) * soft_scale + bias[...]
            top = jnp.max(scores, axis=0, keepdims=True)
            e = jnp.exp(scores - top)
            total = jnp.sum(e, axis=0, keepdims=True)
            prob = e * (1.0 / total)
            weights = prob.astype(BF16)
            grad_prob = mm(values, g, 1, 1)
            delta = jnp.sum(weights.astype(F32) * grad_prob, axis=0, keepdims=True)
            ds = (prob * (grad_prob - delta) * soft_scale).astype(BF16)
            sdq_ref[:, at] = mm(ds, keys, 0, 0).astype(BF16)
            dk_acc[c, :, sl] = mm(ds[REACH * rows:], q, 1, 0)
            dv_acc[c, :, sl] = mm(weights[REACH * rows:], g, 1, 0)
            lse_rows.append(top + jnp.log(total))
            delta_rows.append(delta)
        pad = [jnp.zeros((8 - 2 * per, rows), F32)] if 2 * per < 8 else []
        stat[0, c] = jnp.concatenate(lse_rows + delta_rows + pad, axis=0)
        for j in range(1, REACH + 1):
            @pl.when(b - j >= 0)
            def _():
                stat_move(j, c, b - j).start()

        row_sum = loss_row[0:1, :]
        for h in range(per):
            sl = slice(h * HD, (h + 1) * HD)
            at = pl.ds(pl.multiple_of(c * wide + h * HD, HD), HD)
            g = bwd[0, c, 1, :, sl]
            lq, lk, lv = lq_ref[:, at], lk_ref[:, at], lv_ref[:, at]
            within = bias[REACH * rows:, :] == 0.0
            fore = jnp.where(within, lin_scale * mm(lk, lq, 1, 1), 0.0)
            back_raw = jnp.where(within, mm(lv, g, 1, 1), 0.0)
            row_sum = row_sum + jnp.sum(fore * back_raw, axis=0, keepdims=True) + delta_rows[h]
            fore = fore.astype(BF16)
            back = (lin_scale * back_raw).astype(BF16)
            prior = jnp.zeros((HD, HD), F32)
            later = jnp.zeros((HD, HD), F32)
            for j in range(1, REACH + 1):
                prior = prior + jnp.where(
                    begin_first < pos0 - (j - 1) * rows, 1.0, 0.0
                ) * fwd[j, c, 2, :, sl].astype(F32)
                later = later + jnp.where(
                    end_last > pos0 + j * rows, 1.0, 0.0
                ) * bwd[j, c, 2, :, sl].astype(F32)
            prior = prior.astype(BF16)
            later = later.astype(BF16)
            cross = carried_s[...] * mm(g, prior, 1, 1)
            loss_lane[...] += lq.astype(F32) * cross
            ldq_ref[:, at] = (mm(back, lk, 0, 0) + cross).astype(BF16)
            ext = extended_s[...]
            ldk_ref[:, at] = (mm(back, lq, 1, 0) + ext * mm(lv, later, 1, 1)).astype(BF16)
            ldv_ref[:, at] = (mm(fore, g, 1, 0) + ext * mm(lk, later, 1, 0)).astype(BF16)
        loss_row[0:1, :] = row_sum

    def backward(c):
        for j in range(1, REACH + 1):
            @pl.when(b + j < n_ctx)
            def _():
                stat_move(j, c, partner).wait_recv()
        for h in range(per):
            sl = slice(h * HD, (h + 1) * HD)
            at = pl.ds(pl.multiple_of(c * wide + h * HD, HD), HD)
            k, v = fwd[0, c, 0, :, sl], fwd[0, c, 1, :, sl]
            q = jnp.concatenate([bwd[j, c, 0, :, sl] for j in (1, 2, 3)], axis=0)
            g = jnp.concatenate([bwd[j, c, 1, :, sl] for j in (1, 2, 3)], axis=0)
            lse = jnp.concatenate([stat[j, c, h:h + 1, :] for j in (1, 2, 3)], axis=1)
            delta = jnp.concatenate(
                [stat[j, c, per + h:per + h + 1, :] for j in (1, 2, 3)], axis=1
            )
            prob = jnp.exp(mm(k, q, 1, 1) * soft_scale + bias_later[...] - lse)
            weights = prob.astype(BF16)
            ds = (prob * (mm(v, g, 1, 1) - delta) * soft_scale).astype(BF16)
            sdk_ref[:, at] = (dk_acc[c, :, sl] + mm(ds, q, 1, 0)).astype(BF16)
            sdv_ref[:, at] = (dv_acc[c, :, sl] + mm(weights, g, 1, 0)).astype(BF16)

    def ctx_loss(k):
        return pltpu.make_async_remote_copy(
            src_ref=loss_ctx.at[b],
            dst_ref=loss_ctx.at[b],
            send_sem=send_c.at[k],
            recv_sem=recv_c.at[b],
            device_id={"ctx": lax.rem(b + k, n_ctx)},
            device_id_type=MESH,
        )

    def ctx_arrival(k):
        origin = lax.rem(b + k, n_ctx)
        return pltpu.make_async_remote_copy(
            src_ref=loss_ctx.at[origin],
            dst_ref=loss_ctx.at[origin],
            send_sem=send_c.at[k],
            recv_sem=recv_c.at[origin],
            device_id={"ctx": origin},
            device_id_type=MESH,
        )

    def head_loss(k):
        return pltpu.make_async_remote_copy(
            src_ref=loss_head.at[hd],
            dst_ref=loss_head.at[hd],
            send_sem=send_h.at[k],
            recv_sem=recv_h.at[hd],
            device_id={"head": lax.rem(hd + k, n_head)},
            device_id_type=MESH,
        )

    def head_arrival(k):
        origin = lax.rem(hd + k, n_head)
        return pltpu.make_async_remote_copy(
            src_ref=loss_head.at[origin],
            dst_ref=loss_head.at[origin],
            send_sem=send_h.at[k],
            recv_sem=recv_h.at[origin],
            device_id={"head": origin},
            device_id_type=MESH,
        )

    stage_own(0)
    pl.semaphore_wait(barrier, n_ctx - 1 + n_head - 1)
    send_own(0)

    @pl.loop(1, chunks)
    def _(c):
        stage_own(c)
        send_own(c)

    @pl.loop(0, chunks + 2)
    def _(i):
        @pl.when(i < chunks)
        def _():
            pass_across(i)

        @pl.when((i >= 1) & (i < chunks + 1))
        def _():
            pass_on(i - 1)

        @pl.when(i >= 3)
        def _():
            backward(i - 3)

        @pl.when(i >= 2)
        def _():
            forward(i - 2)

    lane_part = lax.dot_general(
        jnp.ones((8, HD), F32), loss_lane[...], (((1,), (1,)), ((), ())),
        precision=lax.Precision.HIGHEST, preferred_element_type=F32,
    )
    per_token = loss_row[0:1, :] + lane_part[0:1, :]
    domain_id = lax.broadcasted_iota(jnp.int32, (n_dom, rows), 0)
    loss_ctx[b] = jnp.where(dom_s[...] == domain_id, per_token, 0.0)
    for k in range(1, n_ctx):
        ctx_loss(k).start()
    backward(chunks - 1)
    for k in range(1, n_ctx):
        ctx_arrival(k).wait_recv()
    loss_head[hd] = jnp.sum(loss_ctx[...], axis=0)
    for k in range(1, n_head):
        head_loss(k).start()

    @pl.loop(0, chunks)
    def _(c):
        @pl.when(has_up)
        def _():
            f_move(0, c, 0, 2, up2).wait_send()

        @pl.when(has_down)
        def _():
            b_move(0, c, 0, 2, down2).wait_send()

        @pl.when((side == 0) | has_down)
        def _():
            f_move(1, c, 0, 1, partner).wait_send()

        @pl.when((side == 1) | has_up)
        def _():
            b_move(1, c, 0, 1, partner).wait_send()

        @pl.when((b >= 1) & has_up)
        def _():
            f_move(2, c, 1, 3, up2).wait_send()

        @pl.when((b + 1 < n_ctx) & has_down)
        def _():
            b_move(2, c, 1, 3, down2).wait_send()

        for j in range(1, REACH + 1):
            @pl.when(b - j >= 0)
            def _():
                stat_move(j, c, b - j).wait_send()

    for k in range(1, n_ctx):
        ctx_loss(k).wait_send()
    for k in range(1, n_head):
        head_arrival(k).wait_recv()
    loss_ref[...] = jnp.broadcast_to(
        jnp.sum(jnp.sum(loss_head[...], axis=0), axis=1, keepdims=True), loss_ref.shape
    )
    for k in range(1, n_head):
        head_loss(k).wait_send()


def solution(mesh):
    n_ctx, n_head = mesh.shape["ctx"], mesh.shape["head"]

    def on_device(*args):
        rows, cols = args[0].shape
        n_dom = args[9].shape[0]
        wide = HEADS_CHUNK * HD
        chunks = cols // wide
        slots = REACH + 1
        big = jax.ShapeDtypeStruct((rows, cols), BF16)
        vmem = pl.BlockSpec(memory_space=pltpu.VMEM)
        smem = pl.BlockSpec(memory_space=pltpu.SMEM)
        dma = pltpu.SemaphoreType.DMA
        out = pl.pallas_call(
            functools.partial(kernel, n_ctx, n_head),
            out_shape=[big] * 6 + [jax.ShapeDtypeStruct((n_dom, HD), F32)],
            in_specs=[vmem] * 7 + [smem] * 3,
            out_specs=[vmem] * 7,
            scratch_shapes=[
                pltpu.VMEM((slots, chunks, 3, rows, wide), BF16),
                pltpu.VMEM((slots, chunks, 3, rows, wide), BF16),
                pltpu.VMEM((slots, chunks, 8, rows), F32),
                pltpu.VMEM((slots * rows, rows), F32),
                pltpu.VMEM((rows, REACH * rows), F32),
                pltpu.VMEM((8, rows), jnp.int32),
                pltpu.VMEM((8, rows), jnp.int32),
                pltpu.VMEM((rows, HD), F32),
                pltpu.VMEM((rows, HD), F32),
                pltpu.VMEM((rows, HD), F32),
                pltpu.VMEM((chunks, rows, wide), F32),
                pltpu.VMEM((chunks, rows, wide), F32),
                pltpu.VMEM((8, rows), F32),
                pltpu.VMEM((rows, HD), F32),
                pltpu.VMEM((n_ctx, n_dom, rows), F32),
                pltpu.VMEM((n_head, n_dom, rows), F32),
                dma((3, chunks)), dma((slots, chunks)),
                dma((3, chunks)), dma((slots, chunks)),
                dma((slots, chunks)), dma((slots, chunks)),
                dma((n_ctx,)), dma((n_ctx,)),
                dma((n_head,)), dma((n_head,)),
            ],
            compiler_params=pltpu.CompilerParams(
                collective_id=0, has_side_effects=True, vmem_limit_bytes=48 * 1024 * 1024
            ),
        )(*args)
        return tuple(out[:6]) + (out[6][:, 0],)

    spec = P("ctx", "head")
    return jax.shard_map(
        on_device,
        mesh=mesh,
        in_specs=(spec,) * 7 + (P(),) * 3,
        out_specs=(spec,) * 6 + (P(),),
        check_vma=False,
    )
```

```python
import functools

import jax
import jax.numpy as jnp
from jax import lax
from jax.experimental import pallas as pl
from jax.experimental.pallas import tpu as pltpu
from jax.sharding import PartitionSpec as P

HD = 128
DOC_MOST = 384
REACH = 3
HEADS_CHUNK = 1
AHEAD = 3
NEG = -1e30
F32 = jnp.float32
BF16 = jnp.bfloat16
MESH = pl.DeviceIdType.MESH


def mm(a, b, ca, cb):
    return lax.dot_general(a, b, (((ca,), (cb,)), ((), ())), preferred_element_type=F32)


def kernel(
    n_ctx, n_head,
    lq_hbm, lk_hbm, lv_hbm, sq_hbm, sk_hbm, sv_hbm, up_hbm, len_hbm, dom_hbm, dw_hbm,
    ldq_hbm, ldk_hbm, ldv_hbm, sdq_hbm, sdk_hbm, sdv_hbm, loss_ref,
    len_ref, dom_ref, dw_ref, local, result,
    fwd, bwd, stat, bias, bias_later, dom_s, w_s, carried_s, extended_s,
    dk_acc, dv_acc, loss_row, loss_lane, loss_ctx, loss_head,
    send_f, recv_f, send_b, recv_b, send_s, recv_s, send_c, recv_c, send_h, recv_h,
    in_sem, out_sem, doc_sem,
):
    rows, cols = lq_hbm.shape
    chunks = fwd.shape[1]
    wide = fwd.shape[4]
    per = wide // HD
    n_docs = len_ref.shape[0]
    n_dom = dw_ref.shape[0]
    lin_scale = (HD * DOC_MOST) ** (-0.5)
    soft_scale = HD ** (-0.5)
    b = lax.axis_index("ctx")
    hd = lax.axis_index("head")
    side = lax.rem(b, 2)
    partner = b + 1 - 2 * side

    barrier = pltpu.get_barrier_semaphore()
    for k in range(1, n_ctx):
        pl.semaphore_signal(
            barrier, inc=1, device_id={"ctx": lax.rem(b + k, n_ctx)}, device_id_type=MESH
        )
    for k in range(1, n_head):
        pl.semaphore_signal(
            barrier, inc=1, device_id={"head": lax.rem(hd + k, n_head)}, device_id_type=MESH
        )

    doc_copies = [
        pltpu.make_async_copy(source, target, doc_sem.at[n])
        for n, (source, target) in enumerate(
            ((len_hbm, len_ref), (dom_hbm, dom_ref), (dw_hbm, dw_ref))
        )
    ]
    for copy in doc_copies:
        copy.start()

    def fetches(c):
        at = pl.ds(pl.multiple_of(c * wide, HD), wide)
        pairs = (
            (up_hbm, local.at[3, c]),
            (lk_hbm, local.at[1, c]),
            (lv_hbm, local.at[2, c]),
            (lq_hbm, local.at[0, c]),
            (sk_hbm, fwd.at[0, c, 0]),
            (sv_hbm, fwd.at[0, c, 1]),
            (sq_hbm, bwd.at[0, c, 0]),
        )
        return [
            pltpu.make_async_copy(source.at[:, at], target, in_sem.at[n, c])
            for n, (source, target) in enumerate(pairs)
        ]

    def stores(c, which):
        at = pl.ds(pl.multiple_of(c * wide, HD), wide)
        targets = (ldq_hbm, ldk_hbm, ldv_hbm, sdq_hbm, sdk_hbm, sdv_hbm)
        return [
            pltpu.make_async_copy(result.at[n, c], targets[n].at[:, at], out_sem.at[n, c])
            for n in which
        ]

    for c in range(AHEAD):
        for copy in fetches(c):
            copy.start()
    for copy in doc_copies:
        copy.wait()

    pos0 = b * rows
    pos_row = pos0 + lax.broadcasted_iota(jnp.int32, (8, rows), 1)
    pos_col = pos0 + lax.broadcasted_iota(jnp.int32, (rows, HD), 0)
    last = pos0 + rows - 1
    zero = jnp.int32(0)
    begin_row, dom_row = jnp.zeros_like(pos_row), jnp.zeros_like(pos_row)
    begin_col, end_col = jnp.zeros_like(pos_col), jnp.zeros_like(pos_col)
    w_col = jnp.zeros(pos_col.shape, F32)
    begin_first, end_first, begin_last, end_last = zero, zero, zero, zero
    start = zero
    for d in range(n_docs):
        end = start + len_ref[d]
        domain = dom_ref[d]
        weight = dw_ref[domain]
        in_row = (pos_row >= start) & (pos_row < end)
        in_col = (pos_col >= start) & (pos_col < end)
        begin_row = jnp.where(in_row, start, begin_row)
        dom_row = jnp.where(in_row, domain, dom_row)
        begin_col = jnp.where(in_col, start, begin_col)
        end_col = jnp.where(in_col, end, end_col)
        w_col = jnp.where(in_col, weight, w_col)
        has_first = (start <= pos0) & (pos0 < end)
        has_last = (start <= last) & (last < end)
        begin_first = jnp.where(has_first, start, begin_first)
        end_first = jnp.where(has_first, end, end_first)
        begin_last = jnp.where(has_last, start, begin_last)
        end_last = jnp.where(has_last, end, end_last)
        start = end
    dom_s[...] = dom_row
    w_s[...] = w_col
    carried_s[...] = jnp.where(begin_col < pos0, lin_scale, 0.0).astype(F32)
    extended_s[...] = jnp.where(end_col > pos0 + rows, lin_scale, 0.0).astype(F32)
    last_doc = jnp.where(pos_col >= begin_last, 1.0, 0.0).astype(BF16)
    first_doc = jnp.where(pos_col < end_first, 1.0, 0.0).astype(BF16)
    key_pos = pos0 - REACH * rows + lax.broadcasted_iota(jnp.int32, ((REACH + 1) * rows, rows), 0)
    allowed = (key_pos >= begin_row[0:1, :]) & (key_pos <= pos_row[0:1, :])
    bias[...] = jnp.where(allowed, 0.0, NEG).astype(F32)
    for j in range(1, REACH + 1):
        query_pos = pos0 + j * rows + lax.broadcasted_iota(jnp.int32, (rows, rows), 1)
        bias_later[:, (j - 1) * rows:j * rows] = jnp.where(
            query_pos < end_col, 0.0, NEG
        ).astype(F32)
    loss_row[...] = jnp.zeros_like(loss_row)
    loss_lane[...] = jnp.zeros_like(loss_lane)

    for j in range(1, REACH + 1):
        @pl.when(b - j < 0)
        def _():
            fwd[j] = jnp.zeros(fwd.shape[1:], BF16)

        @pl.when(b + j >= n_ctx)
        def _():
            bwd[j] = jnp.zeros(bwd.shape[1:], BF16)
            stat[j] = jnp.zeros(stat.shape[1:], F32)

    def move(buf, send, recv, msg, c, source, target, device):
        return pltpu.make_async_remote_copy(
            src_ref=buf.at[source, c],
            dst_ref=buf.at[target, c],
            send_sem=send.at[msg, c],
            recv_sem=recv.at[target, c],
            device_id={"ctx": device},
            device_id_type=MESH,
        )

    up2, down2 = b + 2, b - 2
    has_up, has_down = b + 2 < n_ctx, b - 2 >= 0

    def f_move(msg, c, source, target, device):
        return move(fwd, send_f, recv_f, msg, c, source, target, device)

    def b_move(msg, c, source, target, device):
        return move(bwd, send_b, recv_b, msg, c, source, target, device)

    def stat_move(j, c, device):
        return pltpu.make_async_remote_copy(
            src_ref=stat.at[0, c],
            dst_ref=stat.at[j, c],
            send_sem=send_s.at[j, c],
            recv_sem=recv_s.at[j, c],
            device_id={"ctx": device},
            device_id_type=MESH,
        )

    def stage_own(c):
        for copy in fetches(c):
            copy.wait()
        for h in range(per):
            sl = slice(h * HD, (h + 1) * HD)
            g = (w_s[...] * local[3, c, :, sl].astype(F32)).astype(BF16)
            fwd[0, c, 2, :, sl] = mm(
                local[1, c, :, sl] * last_doc, local[2, c, :, sl], 0, 0
            ).astype(BF16)
            bwd[0, c, 1, :, sl] = g
            bwd[0, c, 2, :, sl] = mm(local[0, c, :, sl] * first_doc, g, 0, 0).astype(BF16)

    def send_own(c):
        @pl.when(has_up)
        def _():
            f_move(0, c, 0, 2, up2).start()

        @pl.when(has_down)
        def _():
            b_move(0, c, 0, 2, down2).start()

        @pl.when(side == 0)
        def _():
            f_move(1, c, 0, 1, partner).start()

        @pl.when(side == 1)
        def _():
            b_move(1, c, 0, 1, partner).start()

    def pass_across(c):
        @pl.when(has_down)
        def _():
            f_move(0, c, 0, 2, partner).wait_recv()

            @pl.when(side == 1)
            def _():
                f_move(1, c, 2, 1, partner).start()

        @pl.when(has_up)
        def _():
            b_move(0, c, 0, 2, partner).wait_recv()

            @pl.when(side == 0)
            def _():
                b_move(1, c, 2, 1, partner).start()

    def pass_on(c):
        @pl.when(b >= 1)
        def _():
            f_move(1, c, 0, 1, partner).wait_recv()

            @pl.when(has_up)
            def _():
                f_move(2, c, 1, 3, up2).start()

        @pl.when(b + 1 < n_ctx)
        def _():
            b_move(1, c, 0, 1, partner).wait_recv()

            @pl.when(has_down)
            def _():
                b_move(2, c, 1, 3, down2).start()

    def wait_last(c):
        @pl.when(b >= 3)
        def _():
            f_move(2, c, 1, 3, partner).wait_recv()

        @pl.when(b + 3 < n_ctx)
        def _():
            b_move(2, c, 1, 3, partner).wait_recv()

    def forward(c):
        lse_rows, delta_rows = [], []
        for h in range(per):
            sl = slice(h * HD, (h + 1) * HD)
            keys = jnp.concatenate([fwd[j, c, 0, :, sl] for j in (3, 2, 1, 0)], axis=0)
            values = jnp.concatenate([fwd[j, c, 1, :, sl] for j in (3, 2, 1, 0)], axis=0)
            q = bwd[0, c, 0, :, sl]
            g = bwd[0, c, 1, :, sl]
            scores = mm(keys, q, 1, 1) * soft_scale + bias[...]
            top = jnp.max(scores, axis=0, keepdims=True)
            e = jnp.exp(scores - top)
            total = jnp.sum(e, axis=0, keepdims=True)
            prob = e * (1.0 / total)
            weights = prob.astype(BF16)
            grad_prob = mm(values, g, 1, 1)
            delta = jnp.sum(weights.astype(F32) * grad_prob, axis=0, keepdims=True)
            ds = (prob * (grad_prob - delta) * soft_scale).astype(BF16)
            result[3, c, :, sl] = mm(ds, keys, 0, 0).astype(BF16)
            dk_acc[c, :, sl] = mm(ds[REACH * rows:], q, 1, 0)
            dv_acc[c, :, sl] = mm(weights[REACH * rows:], g, 1, 0)
            lse_rows.append(top + jnp.log(total))
            delta_rows.append(delta)
        pad = [jnp.zeros((8 - 2 * per, rows), F32)] if 2 * per < 8 else []
        stat[0, c] = jnp.concatenate(lse_rows + delta_rows + pad, axis=0)
        row_sum = loss_row[0:1, :]
        for h in range(per):
            sl = slice(h * HD, (h + 1) * HD)
            g = bwd[0, c, 1, :, sl]
            lq, lk, lv = local[0, c, :, sl], local[1, c, :, sl], local[2, c, :, sl]
            within = bias[REACH * rows:, :] == 0.0
            fore = jnp.where(within, lin_scale * mm(lk, lq, 1, 1), 0.0)
            back_raw = jnp.where(within, mm(lv, g, 1, 1), 0.0)
            row_sum = row_sum + jnp.sum(fore * back_raw, axis=0, keepdims=True) + delta_rows[h]
            fore = fore.astype(BF16)
            back = (lin_scale * back_raw).astype(BF16)
            prior = jnp.zeros((HD, HD), F32)
            later = jnp.zeros((HD, HD), F32)
            for j in range(1, REACH + 1):
                prior = prior + jnp.where(
                    begin_first < pos0 - (j - 1) * rows, 1.0, 0.0
                ) * fwd[j, c, 2, :, sl].astype(F32)
                later = later + jnp.where(
                    end_last > pos0 + j * rows, 1.0, 0.0
                ) * bwd[j, c, 2, :, sl].astype(F32)
            prior = prior.astype(BF16)
            later = later.astype(BF16)
            cross = carried_s[...] * mm(g, prior, 1, 1)
            loss_lane[...] += lq.astype(F32) * cross
            result[0, c, :, sl] = (mm(back, lk, 0, 0) + cross).astype(BF16)
            ext = extended_s[...]
            result[1, c, :, sl] = (mm(back, lq, 1, 0) + ext * mm(lv, later, 1, 1)).astype(BF16)
            result[2, c, :, sl] = (mm(fore, g, 1, 0) + ext * mm(lk, later, 1, 0)).astype(BF16)
        loss_row[0:1, :] = row_sum

    def after_forward(c):
        for j in range(1, REACH + 1):
            @pl.when(b - j >= 0)
            def _():
                stat_move(j, c, b - j).start()
        for copy in stores(c, range(4)):
            copy.start()

    def wait_stat(c):
        for j in range(1, REACH + 1):
            @pl.when(b + j < n_ctx)
            def _():
                stat_move(j, c, partner).wait_recv()

    def after_backward(c):
        for copy in stores(c, (4, 5)):
            copy.start()

    def backward(c):
        for h in range(per):
            sl = slice(h * HD, (h + 1) * HD)
            k, v = fwd[0, c, 0, :, sl], fwd[0, c, 1, :, sl]
            q = jnp.concatenate([bwd[j, c, 0, :, sl] for j in (1, 2, 3)], axis=0)
            g = jnp.concatenate([bwd[j, c, 1, :, sl] for j in (1, 2, 3)], axis=0)
            lse = jnp.concatenate([stat[j, c, h:h + 1, :] for j in (1, 2, 3)], axis=1)
            delta = jnp.concatenate(
                [stat[j, c, per + h:per + h + 1, :] for j in (1, 2, 3)], axis=1
            )
            prob = jnp.exp(mm(k, q, 1, 1) * soft_scale + bias_later[...] - lse)
            weights = prob.astype(BF16)
            ds = (prob * (mm(v, g, 1, 1) - delta) * soft_scale).astype(BF16)
            result[4, c, :, sl] = (dk_acc[c, :, sl] + mm(ds, q, 1, 0)).astype(BF16)
            result[5, c, :, sl] = (dv_acc[c, :, sl] + mm(weights, g, 1, 0)).astype(BF16)

    def ctx_loss(k):
        return pltpu.make_async_remote_copy(
            src_ref=loss_ctx.at[b],
            dst_ref=loss_ctx.at[b],
            send_sem=send_c.at[k],
            recv_sem=recv_c.at[b],
            device_id={"ctx": lax.rem(b + k, n_ctx)},
            device_id_type=MESH,
        )

    def ctx_arrival(k):
        origin = lax.rem(b + k, n_ctx)
        return pltpu.make_async_remote_copy(
            src_ref=loss_ctx.at[origin],
            dst_ref=loss_ctx.at[origin],
            send_sem=send_c.at[k],
            recv_sem=recv_c.at[origin],
            device_id={"ctx": origin},
            device_id_type=MESH,
        )

    def head_loss(k):
        return pltpu.make_async_remote_copy(
            src_ref=loss_head.at[hd],
            dst_ref=loss_head.at[hd],
            send_sem=send_h.at[k],
            recv_sem=recv_h.at[hd],
            device_id={"head": lax.rem(hd + k, n_head)},
            device_id_type=MESH,
        )

    def head_arrival(k):
        origin = lax.rem(hd + k, n_head)
        return pltpu.make_async_remote_copy(
            src_ref=loss_head.at[origin],
            dst_ref=loss_head.at[origin],
            send_sem=send_h.at[k],
            recv_sem=recv_h.at[origin],
            device_id={"head": origin},
            device_id_type=MESH,
        )

    stage_own(0)
    pl.semaphore_wait(barrier, n_ctx - 1 + n_head - 1)
    send_own(0)
    for c in range(1, AHEAD):
        stage_own(c)
        send_own(c)

    @pl.loop(AHEAD, chunks)
    def _(c):
        for copy in fetches(c):
            copy.start()

    def step(i, across, onward, ahead, front, behind):
        if across:
            pass_across(i)
        if onward:
            pass_on(i - 1)
        if ahead:
            stage_own(i + AHEAD)
            send_own(i + AHEAD)
        if front:
            wait_last(i - 2)
        if behind:
            wait_stat(i - 3)
        if front:
            forward(i - 2)
        if behind:
            backward(i - 3)
        if front:
            after_forward(i - 2)
        if behind:
            after_backward(i - 3)

    for i in range(3):
        step(i, True, i >= 1, i + AHEAD < chunks, i >= 2, False)

    @pl.loop(3, chunks - AHEAD)
    def _(i):
        step(i, True, True, True, True, True)

    @pl.loop(max(3, chunks - AHEAD), chunks)
    def _(i):
        step(i, True, True, False, True, True)

    step(chunks, False, True, False, True, True)
    step(chunks + 1, False, False, False, True, True)

    lane_part = lax.dot_general(
        jnp.ones((8, HD), F32), loss_lane[...], (((1,), (1,)), ((), ())),
        precision=lax.Precision.HIGHEST, preferred_element_type=F32,
    )
    per_token = loss_row[0:1, :] + lane_part[0:1, :]
    domain_id = lax.broadcasted_iota(jnp.int32, (n_dom, rows), 0)
    loss_ctx[b] = jnp.where(dom_s[...] == domain_id, per_token, 0.0)
    for k in range(1, n_ctx):
        ctx_loss(k).start()
    wait_stat(chunks - 1)
    backward(chunks - 1)
    after_backward(chunks - 1)
    for k in range(1, n_ctx):
        ctx_arrival(k).wait_recv()
    loss_head[hd] = jnp.sum(loss_ctx[...], axis=0)
    for k in range(1, n_head):
        head_loss(k).start()

    @pl.loop(0, chunks)
    def _(c):
        @pl.when(has_up)
        def _():
            f_move(0, c, 0, 2, up2).wait_send()

        @pl.when(has_down)
        def _():
            b_move(0, c, 0, 2, down2).wait_send()

        @pl.when((side == 0) | has_down)
        def _():
            f_move(1, c, 0, 1, partner).wait_send()

        @pl.when((side == 1) | has_up)
        def _():
            b_move(1, c, 0, 1, partner).wait_send()

        @pl.when((b >= 1) & has_up)
        def _():
            f_move(2, c, 1, 3, up2).wait_send()

        @pl.when((b + 1 < n_ctx) & has_down)
        def _():
            b_move(2, c, 1, 3, down2).wait_send()

        for j in range(1, REACH + 1):
            @pl.when(b - j >= 0)
            def _():
                stat_move(j, c, b - j).wait_send()

        for copy in stores(c, range(6)):
            copy.wait()

    for k in range(1, n_ctx):
        ctx_loss(k).wait_send()
    for k in range(1, n_head):
        head_arrival(k).wait_recv()
    loss_ref[...] = lax.dot_general(
        jnp.ones((8, rows), F32), jnp.sum(loss_head[...], axis=0), (((1,), (1,)), ((), ())),
        precision=lax.Precision.HIGHEST, preferred_element_type=F32,
    )[0:1, :]
    for k in range(1, n_head):
        head_loss(k).wait_send()


def finish(*refs):
    sources, targets, sems = refs[:6], refs[6:12], refs[12]
    copies = [
        pltpu.make_async_copy(source, target, sems.at[n])
        for n, (source, target) in enumerate(zip(sources, targets))
    ]
    for copy in copies:
        copy.start()
    for copy in copies:
        copy.wait()


def solution(mesh):
    n_ctx, n_head = mesh.shape["ctx"], mesh.shape["head"]

    def on_device(*args):
        rows, cols = args[0].shape
        n_dom = args[9].shape[0]
        wide = HEADS_CHUNK * HD
        chunks = cols // wide
        slots = REACH + 1
        big = jax.ShapeDtypeStruct((rows, cols), BF16)
        vmem = pl.BlockSpec(memory_space=pltpu.VMEM)
        hbm = pl.BlockSpec(memory_space=pl.ANY)
        dma = pltpu.SemaphoreType.DMA
        out = pl.pallas_call(
            functools.partial(kernel, n_ctx, n_head),
            out_shape=[big] * 6 + [jax.ShapeDtypeStruct((1, n_dom), F32)],
            in_specs=[hbm] * 10,
            out_specs=[hbm] * 6 + [vmem],
            scratch_shapes=[
                pltpu.SMEM(args[7].shape, jnp.int32),
                pltpu.SMEM(args[8].shape, jnp.int32),
                pltpu.SMEM(args[9].shape, F32),
                pltpu.VMEM((4, chunks, rows, wide), BF16),
                pltpu.VMEM((6, chunks, rows, wide), BF16),
                pltpu.VMEM((slots, chunks, 3, rows, wide), BF16),
                pltpu.VMEM((slots, chunks, 3, rows, wide), BF16),
                pltpu.VMEM((slots, chunks, 8, rows), F32),
                pltpu.VMEM((slots * rows, rows), F32),
                pltpu.VMEM((rows, REACH * rows), F32),
                pltpu.VMEM((8, rows), jnp.int32),
                pltpu.VMEM((rows, HD), F32),
                pltpu.VMEM((rows, HD), F32),
                pltpu.VMEM((rows, HD), F32),
                pltpu.VMEM((chunks, rows, wide), F32),
                pltpu.VMEM((chunks, rows, wide), F32),
                pltpu.VMEM((8, rows), F32),
                pltpu.VMEM((rows, HD), F32),
                pltpu.VMEM((n_ctx, n_dom, rows), F32),
                pltpu.VMEM((n_head, n_dom, rows), F32),
                dma((3, chunks)), dma((slots, chunks)),
                dma((3, chunks)), dma((slots, chunks)),
                dma((slots, chunks)), dma((slots, chunks)),
                dma((n_ctx,)), dma((n_ctx,)),
                dma((n_head,)), dma((n_head,)),
                dma((7, chunks)), dma((6, chunks)), dma((3,)),
            ],
            compiler_params=pltpu.CompilerParams(
                collective_id=0, has_side_effects=True, vmem_limit_bytes=56 * 1024 * 1024
            ),
        )(*args)
        done = pl.pallas_call(
            finish,
            out_shape=[big] * 6,
            in_specs=[hbm] * 6,
            out_specs=[hbm] * 6,
            scratch_shapes=[dma((6,))],
            compiler_params=pltpu.CompilerParams(vmem_limit_bytes=60 * 1024 * 1024),
        )(*out[:6])
        return tuple(done) + (out[6].reshape(n_dom),)

    spec = P("ctx", "head")
    return jax.shard_map(
        on_device,
        mesh=mesh,
        in_specs=(spec,) * 7 + (P(),) * 3,
        out_specs=(spec,) * 6 + (P(),),
        check_vma=False,
    )
```

```python
import functools

import jax
import jax.numpy as jnp
from jax import lax
from jax.experimental import pallas as pl
from jax.experimental.pallas import tpu as pltpu
from jax.sharding import PartitionSpec as P

HD = 128
DOC_MOST = 384
REACH = 3
HEADS_CHUNK = 1
AHEAD = 3
NEG = -1e30
F32 = jnp.float32
BF16 = jnp.bfloat16
MESH = pl.DeviceIdType.MESH


def mm(a, b, ca, cb):
    return lax.dot_general(a, b, (((ca,), (cb,)), ((), ())), preferred_element_type=F32)


def kernel(
    n_ctx, n_head,
    lq_hbm, lk_hbm, lv_hbm, sq_hbm, sk_hbm, sv_hbm, up_hbm, len_hbm, dom_hbm, dw_hbm,
    ldq_ref, ldk_ref, ldv_ref, sdq_ref, sdk_ref, sdv_ref, loss_ref,
    len_ref, dom_ref, dw_ref, local,
    fwd, bwd, stat, bias, bias_later, dom_s, w_s, carried_s, extended_s,
    dk_acc, dv_acc, loss_row, loss_lane, loss_ctx, loss_head,
    send_f, recv_f, send_b, recv_b, send_s, recv_s, send_c, recv_c, send_h, recv_h,
    in_sem, doc_sem,
):
    rows, cols = lq_hbm.shape
    chunks = fwd.shape[1]
    wide = fwd.shape[4]
    per = wide // HD
    n_docs = len_ref.shape[0]
    n_dom = dw_ref.shape[0]
    lin_scale = (HD * DOC_MOST) ** (-0.5)
    soft_scale = HD ** (-0.5)
    b = lax.axis_index("ctx")
    hd = lax.axis_index("head")
    side = lax.rem(b, 2)
    partner = b + 1 - 2 * side

    barrier = pltpu.get_barrier_semaphore()
    for k in range(1, n_ctx):
        pl.semaphore_signal(
            barrier, inc=1, device_id={"ctx": lax.rem(b + k, n_ctx)}, device_id_type=MESH
        )
    for k in range(1, n_head):
        pl.semaphore_signal(
            barrier, inc=1, device_id={"head": lax.rem(hd + k, n_head)}, device_id_type=MESH
        )

    doc_copies = [
        pltpu.make_async_copy(source, target, doc_sem.at[n])
        for n, (source, target) in enumerate(
            ((len_hbm, len_ref), (dom_hbm, dom_ref), (dw_hbm, dw_ref))
        )
    ]
    for copy in doc_copies:
        copy.start()

    def fetches(c):
        at = pl.ds(pl.multiple_of(c * wide, HD), wide)
        pairs = (
            (up_hbm, local.at[3, c]),
            (lk_hbm, local.at[1, c]),
            (lv_hbm, local.at[2, c]),
            (lq_hbm, local.at[0, c]),
            (sk_hbm, fwd.at[0, c, 0]),
            (sv_hbm, fwd.at[0, c, 1]),
            (sq_hbm, bwd.at[0, c, 0]),
        )
        return [
            pltpu.make_async_copy(source.at[:, at], target, in_sem.at[n, c])
            for n, (source, target) in enumerate(pairs)
        ]

    for c in range(AHEAD):
        for copy in fetches(c):
            copy.start()
    for copy in doc_copies:
        copy.wait()

    pos0 = b * rows
    pos_row = pos0 + lax.broadcasted_iota(jnp.int32, (8, rows), 1)
    pos_col = pos0 + lax.broadcasted_iota(jnp.int32, (rows, HD), 0)
    last = pos0 + rows - 1
    zero = jnp.int32(0)
    begin_row, dom_row = jnp.zeros_like(pos_row), jnp.zeros_like(pos_row)
    begin_col, end_col = jnp.zeros_like(pos_col), jnp.zeros_like(pos_col)
    w_col = jnp.zeros(pos_col.shape, F32)
    begin_first, end_first, begin_last, end_last = zero, zero, zero, zero
    start = zero
    for d in range(n_docs):
        end = start + len_ref[d]
        domain = dom_ref[d]
        weight = dw_ref[domain]
        in_row = (pos_row >= start) & (pos_row < end)
        in_col = (pos_col >= start) & (pos_col < end)
        begin_row = jnp.where(in_row, start, begin_row)
        dom_row = jnp.where(in_row, domain, dom_row)
        begin_col = jnp.where(in_col, start, begin_col)
        end_col = jnp.where(in_col, end, end_col)
        w_col = jnp.where(in_col, weight, w_col)
        has_first = (start <= pos0) & (pos0 < end)
        has_last = (start <= last) & (last < end)
        begin_first = jnp.where(has_first, start, begin_first)
        end_first = jnp.where(has_first, end, end_first)
        begin_last = jnp.where(has_last, start, begin_last)
        end_last = jnp.where(has_last, end, end_last)
        start = end
    dom_s[...] = dom_row
    w_s[...] = w_col
    carried_s[...] = jnp.where(begin_col < pos0, lin_scale, 0.0).astype(F32)
    extended_s[...] = jnp.where(end_col > pos0 + rows, lin_scale, 0.0).astype(F32)
    last_doc = jnp.where(pos_col >= begin_last, 1.0, 0.0).astype(BF16)
    first_doc = jnp.where(pos_col < end_first, 1.0, 0.0).astype(BF16)
    key_pos = pos0 - REACH * rows + lax.broadcasted_iota(jnp.int32, ((REACH + 1) * rows, rows), 0)
    allowed = (key_pos >= begin_row[0:1, :]) & (key_pos <= pos_row[0:1, :])
    bias[...] = jnp.where(allowed, 0.0, NEG).astype(F32)
    for j in range(1, REACH + 1):
        query_pos = pos0 + j * rows + lax.broadcasted_iota(jnp.int32, (rows, rows), 1)
        bias_later[:, (j - 1) * rows:j * rows] = jnp.where(
            query_pos < end_col, 0.0, NEG
        ).astype(F32)
    loss_row[...] = jnp.zeros_like(loss_row)
    loss_lane[...] = jnp.zeros_like(loss_lane)

    for j in range(1, REACH + 1):
        @pl.when(b - j < 0)
        def _():
            fwd[j] = jnp.zeros(fwd.shape[1:], BF16)

        @pl.when(b + j >= n_ctx)
        def _():
            bwd[j] = jnp.zeros(bwd.shape[1:], BF16)
            stat[j] = jnp.zeros(stat.shape[1:], F32)

    def move(buf, send, recv, msg, c, source, target, device):
        return pltpu.make_async_remote_copy(
            src_ref=buf.at[source, c],
            dst_ref=buf.at[target, c],
            send_sem=send.at[msg, c],
            recv_sem=recv.at[target, c],
            device_id={"ctx": device},
            device_id_type=MESH,
        )

    up2, down2 = b + 2, b - 2
    has_up, has_down = b + 2 < n_ctx, b - 2 >= 0

    def f_move(msg, c, source, target, device):
        return move(fwd, send_f, recv_f, msg, c, source, target, device)

    def b_move(msg, c, source, target, device):
        return move(bwd, send_b, recv_b, msg, c, source, target, device)

    def stat_move(j, c, device):
        return pltpu.make_async_remote_copy(
            src_ref=stat.at[0, c],
            dst_ref=stat.at[j, c],
            send_sem=send_s.at[j, c],
            recv_sem=recv_s.at[j, c],
            device_id={"ctx": device},
            device_id_type=MESH,
        )

    def at(c, h):
        return pl.ds(pl.multiple_of(c * wide + h * HD, HD), HD)

    def stage_own(c):
        for copy in fetches(c):
            copy.wait()
        for h in range(per):
            sl = slice(h * HD, (h + 1) * HD)
            g = (w_s[...] * local[3, c, :, sl].astype(F32)).astype(BF16)
            fwd[0, c, 2, :, sl] = mm(
                local[1, c, :, sl] * last_doc, local[2, c, :, sl], 0, 0
            ).astype(BF16)
            bwd[0, c, 1, :, sl] = g
            bwd[0, c, 2, :, sl] = mm(local[0, c, :, sl] * first_doc, g, 0, 0).astype(BF16)

    def send_own(c):
        @pl.when(has_up)
        def _():
            f_move(0, c, 0, 2, up2).start()

        @pl.when(has_down)
        def _():
            b_move(0, c, 0, 2, down2).start()

        @pl.when(side == 0)
        def _():
            f_move(1, c, 0, 1, partner).start()

        @pl.when(side == 1)
        def _():
            b_move(1, c, 0, 1, partner).start()

    def pass_across(c):
        @pl.when(has_down)
        def _():
            f_move(0, c, 0, 2, partner).wait_recv()

            @pl.when(side == 1)
            def _():
                f_move(1, c, 2, 1, partner).start()

        @pl.when(has_up)
        def _():
            b_move(0, c, 0, 2, partner).wait_recv()

            @pl.when(side == 0)
            def _():
                b_move(1, c, 2, 1, partner).start()

    def pass_on(c):
        @pl.when(b >= 1)
        def _():
            f_move(1, c, 0, 1, partner).wait_recv()

            @pl.when(has_up)
            def _():
                f_move(2, c, 1, 3, up2).start()

        @pl.when(b + 1 < n_ctx)
        def _():
            b_move(1, c, 0, 1, partner).wait_recv()

            @pl.when(has_down)
            def _():
                b_move(2, c, 1, 3, down2).start()

    def wait_last(c):
        @pl.when(b >= 3)
        def _():
            f_move(2, c, 1, 3, partner).wait_recv()

        @pl.when(b + 3 < n_ctx)
        def _():
            b_move(2, c, 1, 3, partner).wait_recv()

    def forward(c):
        lse_rows, delta_rows = [], []
        for h in range(per):
            sl = slice(h * HD, (h + 1) * HD)
            keys = jnp.concatenate([fwd[j, c, 0, :, sl] for j in (3, 2, 1, 0)], axis=0)
            values = jnp.concatenate([fwd[j, c, 1, :, sl] for j in (3, 2, 1, 0)], axis=0)
            q = bwd[0, c, 0, :, sl]
            g = bwd[0, c, 1, :, sl]
            scores = mm(keys, q, 1, 1) * soft_scale + bias[...]
            top = jnp.max(scores, axis=0, keepdims=True)
            e = jnp.exp(scores - top)
            total = jnp.sum(e, axis=0, keepdims=True)
            prob = e * (1.0 / total)
            weights = prob.astype(BF16)
            grad_prob = mm(values, g, 1, 1)
            delta = jnp.sum(weights.astype(F32) * grad_prob, axis=0, keepdims=True)
            ds = (prob * (grad_prob - delta) * soft_scale).astype(BF16)
            sdq_ref[:, at(c, h)] = mm(ds, keys, 0, 0).astype(BF16)
            dk_acc[c, :, sl] = mm(ds[REACH * rows:], q, 1, 0)
            dv_acc[c, :, sl] = mm(weights[REACH * rows:], g, 1, 0)
            lse_rows.append(top + jnp.log(total))
            delta_rows.append(delta)
        pad = [jnp.zeros((8 - 2 * per, rows), F32)] if 2 * per < 8 else []
        stat[0, c] = jnp.concatenate(lse_rows + delta_rows + pad, axis=0)
        row_sum = loss_row[0:1, :]
        for h in range(per):
            sl = slice(h * HD, (h + 1) * HD)
            g = bwd[0, c, 1, :, sl]
            lq, lk, lv = local[0, c, :, sl], local[1, c, :, sl], local[2, c, :, sl]
            within = bias[REACH * rows:, :] == 0.0
            fore = jnp.where(within, lin_scale * mm(lk, lq, 1, 1), 0.0)
            back_raw = jnp.where(within, mm(lv, g, 1, 1), 0.0)
            row_sum = row_sum + jnp.sum(fore * back_raw, axis=0, keepdims=True) + delta_rows[h]
            fore = fore.astype(BF16)
            back = (lin_scale * back_raw).astype(BF16)
            prior = jnp.zeros((HD, HD), F32)
            later = jnp.zeros((HD, HD), F32)
            for j in range(1, REACH + 1):
                prior = prior + jnp.where(
                    begin_first < pos0 - (j - 1) * rows, 1.0, 0.0
                ) * fwd[j, c, 2, :, sl].astype(F32)
                later = later + jnp.where(
                    end_last > pos0 + j * rows, 1.0, 0.0
                ) * bwd[j, c, 2, :, sl].astype(F32)
            prior = prior.astype(BF16)
            later = later.astype(BF16)
            cross = carried_s[...] * mm(g, prior, 1, 1)
            loss_lane[...] += lq.astype(F32) * cross
            ldq_ref[:, at(c, h)] = (mm(back, lk, 0, 0) + cross).astype(BF16)
            ext = extended_s[...]
            ldk_ref[:, at(c, h)] = (mm(back, lq, 1, 0) + ext * mm(lv, later, 1, 1)).astype(BF16)
            ldv_ref[:, at(c, h)] = (mm(fore, g, 1, 0) + ext * mm(lk, later, 1, 0)).astype(BF16)
        loss_row[0:1, :] = row_sum

    def after_forward(c):
        for j in range(1, REACH + 1):
            @pl.when(b - j >= 0)
            def _():
                stat_move(j, c, b - j).start()

    def wait_stat(c):
        for j in range(1, REACH + 1):
            @pl.when(b + j < n_ctx)
            def _():
                stat_move(j, c, partner).wait_recv()

    def backward(c):
        for h in range(per):
            sl = slice(h * HD, (h + 1) * HD)
            k, v = fwd[0, c, 0, :, sl], fwd[0, c, 1, :, sl]
            q = jnp.concatenate([bwd[j, c, 0, :, sl] for j in (1, 2, 3)], axis=0)
            g = jnp.concatenate([bwd[j, c, 1, :, sl] for j in (1, 2, 3)], axis=0)
            lse = jnp.concatenate([stat[j, c, h:h + 1, :] for j in (1, 2, 3)], axis=1)
            delta = jnp.concatenate(
                [stat[j, c, per + h:per + h + 1, :] for j in (1, 2, 3)], axis=1
            )
            prob = jnp.exp(mm(k, q, 1, 1) * soft_scale + bias_later[...] - lse)
            weights = prob.astype(BF16)
            ds = (prob * (mm(v, g, 1, 1) - delta) * soft_scale).astype(BF16)
            sdk_ref[:, at(c, h)] = (dk_acc[c, :, sl] + mm(ds, q, 1, 0)).astype(BF16)
            sdv_ref[:, at(c, h)] = (dv_acc[c, :, sl] + mm(weights, g, 1, 0)).astype(BF16)

    def ctx_loss(k):
        return pltpu.make_async_remote_copy(
            src_ref=loss_ctx.at[b],
            dst_ref=loss_ctx.at[b],
            send_sem=send_c.at[k],
            recv_sem=recv_c.at[b],
            device_id={"ctx": lax.rem(b + k, n_ctx)},
            device_id_type=MESH,
        )

    def ctx_arrival(k):
        origin = lax.rem(b + k, n_ctx)
        return pltpu.make_async_remote_copy(
            src_ref=loss_ctx.at[origin],
            dst_ref=loss_ctx.at[origin],
            send_sem=send_c.at[k],
            recv_sem=recv_c.at[origin],
            device_id={"ctx": origin},
            device_id_type=MESH,
        )

    def head_loss(k):
        return pltpu.make_async_remote_copy(
            src_ref=loss_head.at[hd],
            dst_ref=loss_head.at[hd],
            send_sem=send_h.at[k],
            recv_sem=recv_h.at[hd],
            device_id={"head": lax.rem(hd + k, n_head)},
            device_id_type=MESH,
        )

    def head_arrival(k):
        origin = lax.rem(hd + k, n_head)
        return pltpu.make_async_remote_copy(
            src_ref=loss_head.at[origin],
            dst_ref=loss_head.at[origin],
            send_sem=send_h.at[k],
            recv_sem=recv_h.at[origin],
            device_id={"head": origin},
            device_id_type=MESH,
        )

    stage_own(0)
    pl.semaphore_wait(barrier, n_ctx - 1 + n_head - 1)
    send_own(0)
    for c in range(1, AHEAD):
        stage_own(c)
        send_own(c)

    @pl.loop(AHEAD, chunks)
    def _(c):
        for copy in fetches(c):
            copy.start()

    def step(i, across, onward, ahead, front, behind):
        if across:
            pass_across(i)
        if onward:
            pass_on(i - 1)
        if ahead:
            stage_own(i + AHEAD)
            send_own(i + AHEAD)
        if front:
            wait_last(i - 2)
        if behind:
            wait_stat(i - 3)
        if front:
            forward(i - 2)
        if behind:
            backward(i - 3)
        if front:
            after_forward(i - 2)

    for i in range(3):
        step(i, True, i >= 1, i + AHEAD < chunks, i >= 2, False)

    @pl.loop(3, chunks - AHEAD)
    def _(i):
        step(i, True, True, True, True, True)

    @pl.loop(max(3, chunks - AHEAD), chunks)
    def _(i):
        step(i, True, True, False, True, True)

    step(chunks, False, True, False, True, True)
    step(chunks + 1, False, False, False, True, True)

    lane_part = lax.dot_general(
        jnp.ones((8, HD), F32), loss_lane[...], (((1,), (1,)), ((), ())),
        precision=lax.Precision.HIGHEST, preferred_element_type=F32,
    )
    per_token = loss_row[0:1, :] + lane_part[0:1, :]
    domain_id = lax.broadcasted_iota(jnp.int32, (n_dom, rows), 0)
    loss_ctx[b] = jnp.where(dom_s[...] == domain_id, per_token, 0.0)
    for k in range(1, n_ctx):
        ctx_loss(k).start()
    wait_stat(chunks - 1)
    backward(chunks - 1)
    for k in range(1, n_ctx):
        ctx_arrival(k).wait_recv()
    loss_head[hd] = jnp.sum(loss_ctx[...], axis=0)
    for k in range(1, n_head):
        head_loss(k).start()

    @pl.loop(0, chunks)
    def _(c):
        @pl.when(has_up)
        def _():
            f_move(0, c, 0, 2, up2).wait_send()

        @pl.when(has_down)
        def _():
            b_move(0, c, 0, 2, down2).wait_send()

        @pl.when((side == 0) | has_down)
        def _():
            f_move(1, c, 0, 1, partner).wait_send()

        @pl.when((side == 1) | has_up)
        def _():
            b_move(1, c, 0, 1, partner).wait_send()

        @pl.when((b >= 1) & has_up)
        def _():
            f_move(2, c, 1, 3, up2).wait_send()

        @pl.when((b + 1 < n_ctx) & has_down)
        def _():
            b_move(2, c, 1, 3, down2).wait_send()

        for j in range(1, REACH + 1):
            @pl.when(b - j >= 0)
            def _():
                stat_move(j, c, b - j).wait_send()

    for k in range(1, n_ctx):
        ctx_loss(k).wait_send()
    for k in range(1, n_head):
        head_arrival(k).wait_recv()
    loss_ref[...] = lax.dot_general(
        jnp.ones((8, rows), F32), jnp.sum(loss_head[...], axis=0), (((1,), (1,)), ((), ())),
        precision=lax.Precision.HIGHEST, preferred_element_type=F32,
    )[0:1, :]
    for k in range(1, n_head):
        head_loss(k).wait_send()


def finish(*refs):
    sources, targets, held = refs[:7], refs[7:14], refs[14:21]
    in_sem, out_sem = refs[21:]
    loads = [
        pltpu.make_async_copy(source, kept, in_sem.at[n])
        for n, (source, kept) in enumerate(zip(sources, held))
    ]
    saves = [
        pltpu.make_async_copy(kept, target, out_sem.at[n])
        for n, (kept, target) in enumerate(zip(held, targets))
    ]
    for load in loads:
        load.start()
    for load, save in zip(loads, saves):
        load.wait()
        save.start()
    for save in saves:
        save.wait()


def solution(mesh):
    n_ctx, n_head = mesh.shape["ctx"], mesh.shape["head"]

    def on_device(*args):
        rows, cols = args[0].shape
        n_dom = args[9].shape[0]
        wide = HEADS_CHUNK * HD
        chunks = cols // wide
        slots = REACH + 1
        big = jax.ShapeDtypeStruct((rows, cols), BF16)
        vmem = pl.BlockSpec(memory_space=pltpu.VMEM)
        hbm = pl.BlockSpec(memory_space=pl.ANY)
        dma = pltpu.SemaphoreType.DMA
        out = pl.pallas_call(
            functools.partial(kernel, n_ctx, n_head),
            out_shape=[big] * 6 + [jax.ShapeDtypeStruct((1, n_dom), F32)],
            in_specs=[hbm] * 10,
            out_specs=[vmem] * 7,
            scratch_shapes=[
                pltpu.SMEM(args[7].shape, jnp.int32),
                pltpu.SMEM(args[8].shape, jnp.int32),
                pltpu.SMEM(args[9].shape, F32),
                pltpu.VMEM((4, chunks, rows, wide), BF16),
                pltpu.VMEM((slots, chunks, 3, rows, wide), BF16),
                pltpu.VMEM((slots, chunks, 3, rows, wide), BF16),
                pltpu.VMEM((slots, chunks, 8, rows), F32),
                pltpu.VMEM((slots * rows, rows), F32),
                pltpu.VMEM((rows, REACH * rows), F32),
                pltpu.VMEM((8, rows), jnp.int32),
                pltpu.VMEM((rows, HD), F32),
                pltpu.VMEM((rows, HD), F32),
                pltpu.VMEM((rows, HD), F32),
                pltpu.VMEM((chunks, rows, wide), F32),
                pltpu.VMEM((chunks, rows, wide), F32),
                pltpu.VMEM((8, rows), F32),
                pltpu.VMEM((rows, HD), F32),
                pltpu.VMEM((n_ctx, n_dom, rows), F32),
                pltpu.VMEM((n_head, n_dom, rows), F32),
                dma((3, chunks)), dma((slots, chunks)),
                dma((3, chunks)), dma((slots, chunks)),
                dma((slots, chunks)), dma((slots, chunks)),
                dma((n_ctx,)), dma((n_ctx,)),
                dma((n_head,)), dma((n_head,)),
                dma((7, chunks)), dma((3,)),
            ],
            compiler_params=pltpu.CompilerParams(
                collective_id=0, has_side_effects=True, vmem_limit_bytes=56 * 1024 * 1024
            ),
        )(*args)
        done = pl.pallas_call(
            finish,
            out_shape=[big] * 6 + [jax.ShapeDtypeStruct((1, n_dom), F32)],
            in_specs=[hbm] * 7,
            out_specs=[hbm] * 7,
            scratch_shapes=[pltpu.VMEM((rows, cols), BF16)] * 6
            + [pltpu.VMEM((1, n_dom), F32), dma((7,)), dma((7,))],
            compiler_params=pltpu.CompilerParams(vmem_limit_bytes=60 * 1024 * 1024),
        )(*out)
        return tuple(done[:6]) + (done[6].reshape(n_dom),)

    spec = P("ctx", "head")
    return jax.shard_map(
        on_device,
        mesh=mesh,
        in_specs=(spec,) * 7 + (P(),) * 3,
        out_specs=(spec,) * 6 + (P(),),
        check_vma=False,
    )
```

```python
import functools

import jax
import jax.numpy as jnp
from jax import lax
from jax.experimental import pallas as pl
from jax.experimental.pallas import tpu as pltpu
from jax.sharding import PartitionSpec as P

HD = 128
DOC_MOST = 384
REACH = 3
HEADS_CHUNK = 2
AHEAD = 3
NEG = -1e30
F32 = jnp.float32
BF16 = jnp.bfloat16
MESH = pl.DeviceIdType.MESH


def mm(a, b, ca, cb):
    return lax.dot_general(a, b, (((ca,), (cb,)), ((), ())), preferred_element_type=F32)


def kernel(
    n_ctx, n_head,
    lq_hbm, lk_hbm, lv_hbm, sq_hbm, sk_hbm, sv_hbm, up_hbm, len_hbm, dom_hbm, dw_hbm,
    ldq_ref, ldk_ref, ldv_ref, sdq_ref, sdk_ref, sdv_ref, loss_ref,
    len_ref, dom_ref, dw_ref, local,
    fwd, bwd, stat, bias, bias_later, dom_s, w_s, carried_s, extended_s,
    dk_acc, dv_acc, loss_row, loss_lane, loss_ctx, loss_head,
    send_f, recv_f, send_b, recv_b, send_s, recv_s, send_c, recv_c, send_h, recv_h,
    in_sem, doc_sem,
):
    rows, cols = lq_hbm.shape
    chunks = fwd.shape[1]
    wide = fwd.shape[4]
    per = wide // HD
    n_docs = len_ref.shape[0]
    n_dom = dw_ref.shape[0]
    lin_scale = (HD * DOC_MOST) ** (-0.5)
    soft_scale = HD ** (-0.5)
    b = lax.axis_index("ctx")
    hd = lax.axis_index("head")
    side = lax.rem(b, 2)
    partner = b + 1 - 2 * side

    barrier = pltpu.get_barrier_semaphore()
    for k in range(1, n_ctx):
        pl.semaphore_signal(
            barrier, inc=1, device_id={"ctx": lax.rem(b + k, n_ctx)}, device_id_type=MESH
        )
    for k in range(1, n_head):
        pl.semaphore_signal(
            barrier, inc=1, device_id={"head": lax.rem(hd + k, n_head)}, device_id_type=MESH
        )

    doc_copies = [
        pltpu.make_async_copy(source, target, doc_sem.at[n])
        for n, (source, target) in enumerate(
            ((len_hbm, len_ref), (dom_hbm, dom_ref), (dw_hbm, dw_ref))
        )
    ]
    for copy in doc_copies:
        copy.start()

    def fetches(c):
        at = pl.ds(pl.multiple_of(c * wide, HD), wide)
        pairs = (
            (up_hbm, local.at[3, c]),
            (lk_hbm, local.at[1, c]),
            (lv_hbm, local.at[2, c]),
            (lq_hbm, local.at[0, c]),
            (sk_hbm, fwd.at[0, c, 0]),
            (sv_hbm, fwd.at[0, c, 1]),
            (sq_hbm, bwd.at[0, c, 0]),
        )
        return [
            pltpu.make_async_copy(source.at[:, at], target, in_sem.at[n, c])
            for n, (source, target) in enumerate(pairs)
        ]

    for c in range(AHEAD):
        for copy in fetches(c):
            copy.start()
    for copy in doc_copies:
        copy.wait()

    pos0 = b * rows
    pos_row = pos0 + lax.broadcasted_iota(jnp.int32, (8, rows), 1)
    pos_col = pos0 + lax.broadcasted_iota(jnp.int32, (rows, HD), 0)
    last = pos0 + rows - 1
    zero = jnp.int32(0)
    begin_row, dom_row = jnp.zeros_like(pos_row), jnp.zeros_like(pos_row)
    begin_col, end_col = jnp.zeros_like(pos_col), jnp.zeros_like(pos_col)
    w_col = jnp.zeros(pos_col.shape, F32)
    begin_first, end_first, begin_last, end_last = zero, zero, zero, zero
    start = zero
    for d in range(n_docs):
        end = start + len_ref[d]
        domain = dom_ref[d]
        weight = dw_ref[domain]
        in_row = (pos_row >= start) & (pos_row < end)
        in_col = (pos_col >= start) & (pos_col < end)
        begin_row = jnp.where(in_row, start, begin_row)
        dom_row = jnp.where(in_row, domain, dom_row)
        begin_col = jnp.where(in_col, start, begin_col)
        end_col = jnp.where(in_col, end, end_col)
        w_col = jnp.where(in_col, weight, w_col)
        has_first = (start <= pos0) & (pos0 < end)
        has_last = (start <= last) & (last < end)
        begin_first = jnp.where(has_first, start, begin_first)
        end_first = jnp.where(has_first, end, end_first)
        begin_last = jnp.where(has_last, start, begin_last)
        end_last = jnp.where(has_last, end, end_last)
        start = end
    dom_s[...] = dom_row
    w_s[...] = w_col
    carried_s[...] = jnp.where(begin_col < pos0, lin_scale, 0.0).astype(F32)
    extended_s[...] = jnp.where(end_col > pos0 + rows, lin_scale, 0.0).astype(F32)
    last_doc = jnp.where(pos_col >= begin_last, 1.0, 0.0).astype(BF16)
    first_doc = jnp.where(pos_col < end_first, 1.0, 0.0).astype(BF16)
    key_pos = pos0 - REACH * rows + lax.broadcasted_iota(jnp.int32, ((REACH + 1) * rows, rows), 0)
    allowed = (key_pos >= begin_row[0:1, :]) & (key_pos <= pos_row[0:1, :])
    bias[...] = jnp.where(allowed, 0.0, NEG).astype(F32)
    for j in range(1, REACH + 1):
        query_pos = pos0 + j * rows + lax.broadcasted_iota(jnp.int32, (rows, rows), 1)
        bias_later[:, (j - 1) * rows:j * rows] = jnp.where(
            query_pos < end_col, 0.0, NEG
        ).astype(F32)
    loss_row[...] = jnp.zeros_like(loss_row)
    loss_lane[...] = jnp.zeros_like(loss_lane)

    for j in range(1, REACH + 1):
        @pl.when(b - j < 0)
        def _():
            fwd[j] = jnp.zeros(fwd.shape[1:], BF16)

        @pl.when(b + j >= n_ctx)
        def _():
            bwd[j] = jnp.zeros(bwd.shape[1:], BF16)
            stat[j] = jnp.zeros(stat.shape[1:], F32)

    def move(buf, send, recv, msg, c, source, target, device):
        return pltpu.make_async_remote_copy(
            src_ref=buf.at[source, c],
            dst_ref=buf.at[target, c],
            send_sem=send.at[msg, c],
            recv_sem=recv.at[target, c],
            device_id={"ctx": device},
            device_id_type=MESH,
        )

    up2, down2 = b + 2, b - 2
    has_up, has_down = b + 2 < n_ctx, b - 2 >= 0

    def f_move(msg, c, source, target, device):
        return move(fwd, send_f, recv_f, msg, c, source, target, device)

    def b_move(msg, c, source, target, device):
        return move(bwd, send_b, recv_b, msg, c, source, target, device)

    def stat_move(j, c, device):
        return pltpu.make_async_remote_copy(
            src_ref=stat.at[0, c],
            dst_ref=stat.at[j, c],
            send_sem=send_s.at[j, c],
            recv_sem=recv_s.at[j, c],
            device_id={"ctx": device},
            device_id_type=MESH,
        )

    def at(c, h):
        return pl.ds(pl.multiple_of(c * wide + h * HD, HD), HD)

    def stage_own(c):
        for copy in fetches(c):
            copy.wait()
        for h in range(per):
            sl = slice(h * HD, (h + 1) * HD)
            g = (w_s[...] * local[3, c, :, sl].astype(F32)).astype(BF16)
            fwd[0, c, 2, :, sl] = mm(
                local[1, c, :, sl] * last_doc, local[2, c, :, sl], 0, 0
            ).astype(BF16)
            bwd[0, c, 1, :, sl] = g
            bwd[0, c, 2, :, sl] = mm(local[0, c, :, sl] * first_doc, g, 0, 0).astype(BF16)

    def send_own(c):
        @pl.when(has_up)
        def _():
            f_move(0, c, 0, 2, up2).start()

        @pl.when(has_down)
        def _():
            b_move(0, c, 0, 2, down2).start()

        @pl.when(side == 0)
        def _():
            f_move(1, c, 0, 1, partner).start()

        @pl.when(side == 1)
        def _():
            b_move(1, c, 0, 1, partner).start()

    def pass_across(c):
        @pl.when(has_down)
        def _():
            f_move(0, c, 0, 2, partner).wait_recv()

            @pl.when(side == 1)
            def _():
                f_move(1, c, 2, 1, partner).start()

        @pl.when(has_up)
        def _():
            b_move(0, c, 0, 2, partner).wait_recv()

            @pl.when(side == 0)
            def _():
                b_move(1, c, 2, 1, partner).start()

    def pass_on(c):
        @pl.when(b >= 1)
        def _():
            f_move(1, c, 0, 1, partner).wait_recv()

            @pl.when(has_up)
            def _():
                f_move(2, c, 1, 3, up2).start()

        @pl.when(b + 1 < n_ctx)
        def _():
            b_move(1, c, 0, 1, partner).wait_recv()

            @pl.when(has_down)
            def _():
                b_move(2, c, 1, 3, down2).start()

    def wait_last(c):
        @pl.when(b >= 3)
        def _():
            f_move(2, c, 1, 3, partner).wait_recv()

        @pl.when(b + 3 < n_ctx)
        def _():
            b_move(2, c, 1, 3, partner).wait_recv()

    def forward(c):
        lse_rows, delta_rows = [], []
        for h in range(per):
            sl = slice(h * HD, (h + 1) * HD)
            keys = jnp.concatenate([fwd[j, c, 0, :, sl] for j in (3, 2, 1, 0)], axis=0)
            values = jnp.concatenate([fwd[j, c, 1, :, sl] for j in (3, 2, 1, 0)], axis=0)
            q = bwd[0, c, 0, :, sl]
            g = bwd[0, c, 1, :, sl]
            scores = mm(keys, q, 1, 1) * soft_scale + bias[...]
            top = jnp.max(scores, axis=0, keepdims=True)
            e = jnp.exp(scores - top)
            total = jnp.sum(e, axis=0, keepdims=True)
            prob = e * (1.0 / total)
            weights = prob.astype(BF16)
            grad_prob = mm(values, g, 1, 1)
            delta = jnp.sum(weights.astype(F32) * grad_prob, axis=0, keepdims=True)
            ds = (prob * (grad_prob - delta) * soft_scale).astype(BF16)
            sdq_ref[:, at(c, h)] = mm(ds, keys, 0, 0).astype(BF16)
            dk_acc[c, :, sl] = mm(ds[REACH * rows:], q, 1, 0)
            dv_acc[c, :, sl] = mm(weights[REACH * rows:], g, 1, 0)
            lse_rows.append(top + jnp.log(total))
            delta_rows.append(delta)
        pad = [jnp.zeros((8 - 2 * per, rows), F32)] if 2 * per < 8 else []
        stat[0, c] = jnp.concatenate(lse_rows + delta_rows + pad, axis=0)
        row_sum = loss_row[0:1, :]
        for h in range(per):
            sl = slice(h * HD, (h + 1) * HD)
            g = bwd[0, c, 1, :, sl]
            lq, lk, lv = local[0, c, :, sl], local[1, c, :, sl], local[2, c, :, sl]
            within = bias[REACH * rows:, :] == 0.0
            fore = jnp.where(within, lin_scale * mm(lk, lq, 1, 1), 0.0)
            back_raw = jnp.where(within, mm(lv, g, 1, 1), 0.0)
            row_sum = row_sum + jnp.sum(fore * back_raw, axis=0, keepdims=True) + delta_rows[h]
            fore = fore.astype(BF16)
            back = (lin_scale * back_raw).astype(BF16)
            prior = jnp.zeros((HD, HD), F32)
            later = jnp.zeros((HD, HD), F32)
            for j in range(1, REACH + 1):
                prior = prior + jnp.where(
                    begin_first < pos0 - (j - 1) * rows, 1.0, 0.0
                ) * fwd[j, c, 2, :, sl].astype(F32)
                later = later + jnp.where(
                    end_last > pos0 + j * rows, 1.0, 0.0
                ) * bwd[j, c, 2, :, sl].astype(F32)
            prior = prior.astype(BF16)
            later = later.astype(BF16)
            cross = carried_s[...] * mm(g, prior, 1, 1)
            loss_lane[...] += lq.astype(F32) * cross
            ldq_ref[:, at(c, h)] = (mm(back, lk, 0, 0) + cross).astype(BF16)
            ext = extended_s[...]
            ldk_ref[:, at(c, h)] = (mm(back, lq, 1, 0) + ext * mm(lv, later, 1, 1)).astype(BF16)
            ldv_ref[:, at(c, h)] = (mm(fore, g, 1, 0) + ext * mm(lk, later, 1, 0)).astype(BF16)
        loss_row[0:1, :] = row_sum

    def after_forward(c):
        for j in range(1, REACH + 1):
            @pl.when(b - j >= 0)
            def _():
                stat_move(j, c, b - j).start()

    def wait_stat(c):
        for j in range(1, REACH + 1):
            @pl.when(b + j < n_ctx)
            def _():
                stat_move(j, c, partner).wait_recv()

    def backward(c):
        for h in range(per):
            sl = slice(h * HD, (h + 1) * HD)
            k, v = fwd[0, c, 0, :, sl], fwd[0, c, 1, :, sl]
            q = jnp.concatenate([bwd[j, c, 0, :, sl] for j in (1, 2, 3)], axis=0)
            g = jnp.concatenate([bwd[j, c, 1, :, sl] for j in (1, 2, 3)], axis=0)
            lse = jnp.concatenate([stat[j, c, h:h + 1, :] for j in (1, 2, 3)], axis=1)
            delta = jnp.concatenate(
                [stat[j, c, per + h:per + h + 1, :] for j in (1, 2, 3)], axis=1
            )
            prob = jnp.exp(mm(k, q, 1, 1) * soft_scale + bias_later[...] - lse)
            weights = prob.astype(BF16)
            ds = (prob * (mm(v, g, 1, 1) - delta) * soft_scale).astype(BF16)
            sdk_ref[:, at(c, h)] = (dk_acc[c, :, sl] + mm(ds, q, 1, 0)).astype(BF16)
            sdv_ref[:, at(c, h)] = (dv_acc[c, :, sl] + mm(weights, g, 1, 0)).astype(BF16)

    def ctx_loss(k):
        return pltpu.make_async_remote_copy(
            src_ref=loss_ctx.at[b],
            dst_ref=loss_ctx.at[b],
            send_sem=send_c.at[k],
            recv_sem=recv_c.at[b],
            device_id={"ctx": lax.rem(b + k, n_ctx)},
            device_id_type=MESH,
        )

    def ctx_arrival(k):
        origin = lax.rem(b + k, n_ctx)
        return pltpu.make_async_remote_copy(
            src_ref=loss_ctx.at[origin],
            dst_ref=loss_ctx.at[origin],
            send_sem=send_c.at[k],
            recv_sem=recv_c.at[origin],
            device_id={"ctx": origin},
            device_id_type=MESH,
        )

    def head_loss(k):
        return pltpu.make_async_remote_copy(
            src_ref=loss_head.at[hd],
            dst_ref=loss_head.at[hd],
            send_sem=send_h.at[k],
            recv_sem=recv_h.at[hd],
            device_id={"head": lax.rem(hd + k, n_head)},
            device_id_type=MESH,
        )

    def head_arrival(k):
        origin = lax.rem(hd + k, n_head)
        return pltpu.make_async_remote_copy(
            src_ref=loss_head.at[origin],
            dst_ref=loss_head.at[origin],
            send_sem=send_h.at[k],
            recv_sem=recv_h.at[origin],
            device_id={"head": origin},
            device_id_type=MESH,
        )

    stage_own(0)
    pl.semaphore_wait(barrier, n_ctx - 1 + n_head - 1)
    send_own(0)
    for c in range(1, AHEAD):
        stage_own(c)
        send_own(c)

    @pl.loop(AHEAD, chunks)
    def _(c):
        for copy in fetches(c):
            copy.start()

    def step(i, across, onward, ahead, front, behind):
        if across:
            pass_across(i)
        if onward:
            pass_on(i - 1)
        if ahead:
            stage_own(i + AHEAD)
            send_own(i + AHEAD)
        if front:
            wait_last(i - 2)
        if behind:
            wait_stat(i - 3)
        if front:
            forward(i - 2)
        if behind:
            backward(i - 3)
        if front:
            after_forward(i - 2)

    for i in range(3):
        step(i, True, i >= 1, i + AHEAD < chunks, i >= 2, False)

    @pl.loop(3, chunks - AHEAD)
    def _(i):
        step(i, True, True, True, True, True)

    @pl.loop(max(3, chunks - AHEAD), chunks)
    def _(i):
        step(i, True, True, False, True, True)

    step(chunks, False, True, False, True, True)
    step(chunks + 1, False, False, False, True, True)

    lane_part = lax.dot_general(
        jnp.ones((8, HD), F32), loss_lane[...], (((1,), (1,)), ((), ())),
        precision=lax.Precision.HIGHEST, preferred_element_type=F32,
    )
    per_token = loss_row[0:1, :] + lane_part[0:1, :]
    domain_id = lax.broadcasted_iota(jnp.int32, (n_dom, rows), 0)
    loss_ctx[b] = jnp.where(dom_s[...] == domain_id, per_token, 0.0)
    for k in range(1, n_ctx):
        ctx_loss(k).start()
    wait_stat(chunks - 1)
    backward(chunks - 1)
    for k in range(1, n_ctx):
        ctx_arrival(k).wait_recv()
    loss_head[hd] = jnp.sum(loss_ctx[...], axis=0)
    for k in range(1, n_head):
        head_loss(k).start()

    @pl.loop(0, chunks)
    def _(c):
        @pl.when(has_up)
        def _():
            f_move(0, c, 0, 2, up2).wait_send()

        @pl.when(has_down)
        def _():
            b_move(0, c, 0, 2, down2).wait_send()

        @pl.when((side == 0) | has_down)
        def _():
            f_move(1, c, 0, 1, partner).wait_send()

        @pl.when((side == 1) | has_up)
        def _():
            b_move(1, c, 0, 1, partner).wait_send()

        @pl.when((b >= 1) & has_up)
        def _():
            f_move(2, c, 1, 3, up2).wait_send()

        @pl.when((b + 1 < n_ctx) & has_down)
        def _():
            b_move(2, c, 1, 3, down2).wait_send()

        for j in range(1, REACH + 1):
            @pl.when(b - j >= 0)
            def _():
                stat_move(j, c, b - j).wait_send()

    for k in range(1, n_ctx):
        ctx_loss(k).wait_send()
    for k in range(1, n_head):
        head_arrival(k).wait_recv()
    loss_ref[...] = lax.dot_general(
        jnp.ones((8, rows), F32), jnp.sum(loss_head[...], axis=0), (((1,), (1,)), ((), ())),
        precision=lax.Precision.HIGHEST, preferred_element_type=F32,
    )[0:1, :]
    for k in range(1, n_head):
        head_loss(k).wait_send()


def finish(*refs):
    sources, targets, held = refs[:7], refs[7:14], refs[14:21]
    in_sem, out_sem = refs[21:]
    loads = [
        pltpu.make_async_copy(source, kept, in_sem.at[n])
        for n, (source, kept) in enumerate(zip(sources, held))
    ]
    saves = [
        pltpu.make_async_copy(kept, target, out_sem.at[n])
        for n, (kept, target) in enumerate(zip(held, targets))
    ]
    for load in loads:
        load.start()
    for load, save in zip(loads, saves):
        load.wait()
        save.start()
    for save in saves:
        save.wait()


def solution(mesh):
    n_ctx, n_head = mesh.shape["ctx"], mesh.shape["head"]

    def on_device(*args):
        rows, cols = args[0].shape
        n_dom = args[9].shape[0]
        wide = HEADS_CHUNK * HD
        chunks = cols // wide
        slots = REACH + 1
        big = jax.ShapeDtypeStruct((rows, cols), BF16)
        vmem = pl.BlockSpec(memory_space=pltpu.VMEM)
        hbm = pl.BlockSpec(memory_space=pl.ANY)
        dma = pltpu.SemaphoreType.DMA
        out = pl.pallas_call(
            functools.partial(kernel, n_ctx, n_head),
            out_shape=[big] * 6 + [jax.ShapeDtypeStruct((1, n_dom), F32)],
            in_specs=[hbm] * 10,
            out_specs=[vmem] * 7,
            scratch_shapes=[
                pltpu.SMEM(args[7].shape, jnp.int32),
                pltpu.SMEM(args[8].shape, jnp.int32),
                pltpu.SMEM(args[9].shape, F32),
                pltpu.VMEM((4, chunks, rows, wide), BF16),
                pltpu.VMEM((slots, chunks, 3, rows, wide), BF16),
                pltpu.VMEM((slots, chunks, 3, rows, wide), BF16),
                pltpu.VMEM((slots, chunks, 8, rows), F32),
                pltpu.VMEM((slots * rows, rows), F32),
                pltpu.VMEM((rows, REACH * rows), F32),
                pltpu.VMEM((8, rows), jnp.int32),
                pltpu.VMEM((rows, HD), F32),
                pltpu.VMEM((rows, HD), F32),
                pltpu.VMEM((rows, HD), F32),
                pltpu.VMEM((chunks, rows, wide), F32),
                pltpu.VMEM((chunks, rows, wide), F32),
                pltpu.VMEM((8, rows), F32),
                pltpu.VMEM((rows, HD), F32),
                pltpu.VMEM((n_ctx, n_dom, rows), F32),
                pltpu.VMEM((n_head, n_dom, rows), F32),
                dma((3, chunks)), dma((slots, chunks)),
                dma((3, chunks)), dma((slots, chunks)),
                dma((slots, chunks)), dma((slots, chunks)),
                dma((n_ctx,)), dma((n_ctx,)),
                dma((n_head,)), dma((n_head,)),
                dma((7, chunks)), dma((3,)),
            ],
            compiler_params=pltpu.CompilerParams(
                collective_id=0, has_side_effects=True, vmem_limit_bytes=56 * 1024 * 1024
            ),
        )(*args)
        done = pl.pallas_call(
            finish,
            out_shape=[big] * 6 + [jax.ShapeDtypeStruct((1, n_dom), F32)],
            in_specs=[hbm] * 7,
            out_specs=[hbm] * 7,
            scratch_shapes=[pltpu.VMEM((rows, cols), BF16)] * 6
            + [pltpu.VMEM((1, n_dom), F32), dma((7,)), dma((7,))],
            compiler_params=pltpu.CompilerParams(vmem_limit_bytes=60 * 1024 * 1024),
        )(*out)
        return tuple(done[:6]) + (done[6].reshape(n_dom),)

    spec = P("ctx", "head")
    return jax.shard_map(
        on_device,
        mesh=mesh,
        in_specs=(spec,) * 7 + (P(),) * 3,
        out_specs=(spec,) * 6 + (P(),),
        check_vma=False,
    )
```
